128 devices in a mesh: curve: 128 (over y, x, z, core).
Axes of the slice: x: 4, y: 4, z: 4, core: 2. Of those that a mesh axis runs over, the one named last changes fastest.
Arguments:
- multipole: bfloat16 [152, 131072], P(None, 'curve'), may hold values from -6 to 6
- upward_maps: bfloat16 [8, 152, 152], replicated, may hold values from -0.15625 to 0.15625
- transfer_maps: bfloat16 [316, 152, 152], replicated, may hold values from -0.03125 to 0.03125
- downward_maps: bfloat16 [8, 152, 152], replicated, may hold values from -0.5 to 0.5
- check_inverse: bfloat16 [152, 152], replicated, may hold values from -0.5 to 0.5
- fine_lists: int32 [316, 131072], P(None, 'curve'), may hold values from -1 to 1023, as said below
- coarse_lists: int32 [316, 16384], P(None, 'curve'), may hold values from -1 to 127, as said below
Outputs:
- local_density: bfloat16 [152, 131072], P(None, 'curve')
The draws below stay inside these ranges and needn't reach their ends.
Inputs may be any that keep to these rules, and one draw needn't show every extreme that they name: `fine_lists`: entry k of box t is -1 or the place, within its own brick, of the fine box at offset k from t; it is a place only where that box lies in the grid, its parent touches the parent of t, and both boxes are present in the tree. `coarse_lists`: entry k of box t is -1 or the place, within its own brick, of the coarse box at offset k from t; it is a place only where that box lies in the grid, its parent touches the parent of t, and both boxes are present in the tree (a coarse box is present when one of its children is).
All inputs are finite; a program needn't handle non-finite values.
Results may differ from the reference program's by a relative error of at most 0.0055.
Values may be sent and summed in bfloat16 or wider, within the bound.
A program may use at most 704 MiB of HBM per device.

```python
import jax
import jax.numpy as jnp
import numpy as np
from jax import lax

P_SIZE = 152
OFFS = 316
BX = 8
BY = 8
BZ = 16
BOXES = 131072
N_CURVE = 128


SHIFTS = [(first_axis, second_axis, third_axis) for first_axis in range(-3, 4) for second_axis in range(-3, 4) for third_axis in range(-3, 4) if max(abs(first_axis), abs(second_axis), abs(third_axis)) >= 2]


def curve_numbers(brick, devices):
    levels = devices.bit_length() - 1
    limits = (2 ** (levels // 3), 2 ** ((levels + 1) // 3), 2 ** ((levels + 2) // 3))
    numbers = np.arange(devices)
    places = [np.zeros(devices, np.int64) for axis_number in range(3)]
    for bit_place in range(levels):
        places[2 - bit_place % 3] += (numbers >> bit_place & 1) << bit_place // 3
    box_count = brick[0] * brick[1] * brick[2]
    within = np.arange(box_count).reshape(brick)
    numbering = np.zeros((limits[0] * brick[0], limits[1] * brick[1], limits[2] * brick[2]), np.int64)
    for device_number in range(devices):
        corner_x = places[0][device_number] * brick[0]
        corner_y = places[1][device_number] * brick[1]
        corner_z = places[2][device_number] * brick[2]
        numbering[corner_x:corner_x + brick[0], corner_y:corner_y + brick[1], corner_z:corner_z + brick[2]] = device_number * box_count + within
    return numbering


def level_lists(present, numbering, box_count):
    size_x, size_y, size_z = numbering.shape
    padded_present = jnp.pad(present, 3)
    padded_numbers = jnp.pad(jnp.asarray(numbering % box_count, jnp.int32), 3, constant_values=-1)
    coord_lists = (np.arange(size_x)[:, None, None], np.arange(size_y)[None, :, None], np.arange(size_z)[None, None, :])
    rows = []
    for offset in SHIFTS:
        allowed = np.ones(numbering.shape, bool)
        for axis_number in range(3):
            coords = coord_lists[axis_number]
            moved = coords + offset[axis_number]
            allowed = allowed & (moved // 2 - coords // 2 >= -1) & (moved // 2 - coords // 2 <= 1)
        source_present = padded_present[3 + offset[0]:3 + offset[0] + size_x, 3 + offset[1]:3 + offset[1] + size_y, 3 + offset[2]:3 + offset[2] + size_z]
        source_number = padded_numbers[3 + offset[0]:3 + offset[0] + size_x, 3 + offset[1]:3 + offset[1] + size_y, 3 + offset[2]:3 + offset[2] + size_z]
        keeping = jnp.asarray(allowed) & present & source_present
        rows.append(jnp.where(keeping, source_number, -1))
    stacked = jnp.stack(rows).reshape(len(SHIFTS), -1)
    ordering = np.argsort(numbering.ravel())
    return stacked[:, ordering].astype(jnp.int32)


def tree_lists(key):
    tree_key = jax.random.fold_in(key, 4099)
    fine_numbers = curve_numbers((BX, BY, BZ), N_CURVE)
    coarse_numbers = curve_numbers((BX // 2, BY // 2, BZ // 2), N_CURVE)
    size_x, size_y, size_z = coarse_numbers.shape
    fill_rates = jax.random.randint(jax.random.fold_in(tree_key, 1), (size_x, size_y, size_z), 2, 9)
    fill_rates = fill_rates.at[-4:, -4:, -4:].set(8)
    samples = jax.random.randint(jax.random.fold_in(tree_key, 2), (2 * size_x, 2 * size_y, 2 * size_z), 0, 8)
    spread_rates = jnp.repeat(jnp.repeat(jnp.repeat(fill_rates, 2, 0), 2, 1), 2, 2)
    fine_present = samples < spread_rates
    coarse_present = fine_present.reshape(size_x, 2, size_y, 2, size_z, 2).any(axis=(1, 3, 5))
    fine_count = BX * BY * BZ
    return (level_lists(fine_present, fine_numbers, fine_count), level_lists(coarse_present, coarse_numbers, fine_count // 8))


def draw_fine_lists(key, part):
    return tree_lists(key)[0]


def draw_coarse_lists(key, part):
    return tree_lists(key)[1]


def block_levels(stream_key, dims, pieces, low, top_value):
    gain, own = 1.0, jax.random.fold_in(stream_key, 6)
    for axis_at, shards_of in pieces:
        draws = jnp.exp(jax.random.uniform(jax.random.fold_in(own, axis_at), (shards_of,), jnp.float32, low / len(pieces), top_value / len(pieces)))
        gain = gain * jnp.repeat(draws, dims[axis_at] // shards_of).reshape([-1 if axis == axis_at else 1 for axis in range(len(dims))])
    return gain


def noise(own_key, shape, width, reach, split=(), kind=jnp.bfloat16):
    gain = block_levels(own_key, shape, split, -0.22, 0.18) if split else 1.0
    entries = jax.random.normal(own_key, shape, jnp.float32) * width * gain
    return jnp.minimum(jnp.maximum(entries, -reach), reach).astype(kind)


def setup_inputs(seed: int = 0) -> dict:
    seeds = jax.random.split(jax.random.key(seed), 8)
    return {
        "multipole": noise(seeds[0], (P_SIZE, BOXES), 1.0, 6.0, ((1, 128),)),
        "upward_maps": noise(seeds[1], (8, P_SIZE, P_SIZE), (8 * P_SIZE) ** -0.5, 0.15625),
        "transfer_maps": noise(seeds[2], (OFFS, P_SIZE, P_SIZE), (189 * P_SIZE) ** -0.5, 0.03125),
        "downward_maps": noise(seeds[3], (8, P_SIZE, P_SIZE), P_SIZE ** -0.5, 0.5),
        "check_inverse": noise(seeds[4], (P_SIZE, P_SIZE), P_SIZE ** -0.5, 0.5),
        "fine_lists": draw_fine_lists(jax.random.fold_in(seeds[7], 71), 0),
        "coarse_lists": draw_coarse_lists(jax.random.fold_in(seeds[7], 71), 0),
    }


SHIFTS = [(first_axis, second_axis, third_axis) for first_axis in range(-3, 4) for second_axis in range(-3, 4) for third_axis in range(-3, 4) if max(abs(first_axis), abs(second_axis), abs(third_axis)) >= 2]


def curve_layout(devices):
    levels = devices.bit_length() - 1
    limits = (2 ** (levels // 3), 2 ** ((levels + 1) // 3), 2 ** ((levels + 2) // 3))
    numbers = np.arange(devices)
    places = [np.zeros(devices, np.int64) for axis_number in range(3)]
    for bit_place in range(levels):
        places[2 - bit_place % 3] += ((numbers >> bit_place) & 1) << (bit_place // 3)
    lexical = (places[0] * limits[1] + places[1]) * limits[2] + places[2]
    return np.argsort(lexical), limits


def to_grid(flattened, brick, devices):
    lookup, limits = curve_layout(devices)
    leading = flattened.shape[0]
    bricks = flattened.reshape(leading, devices, brick[0], brick[1], brick[2])[:, lookup]
    bricks = bricks.reshape(leading, limits[0], limits[1], limits[2], brick[0], brick[1], brick[2])
    return bricks.transpose(0, 1, 4, 2, 5, 3, 6).reshape(leading, limits[0] * brick[0], limits[1] * brick[1], limits[2] * brick[2])


def from_grid(numbering, brick, devices):
    lookup, limits = curve_layout(devices)
    leading = numbering.shape[0]
    bricks = numbering.reshape(leading, limits[0], brick[0], limits[1], brick[1], limits[2], brick[2])
    bricks = bricks.transpose(0, 1, 3, 5, 2, 4, 6).reshape(leading, devices, brick[0] * brick[1] * brick[2])
    return bricks[:, np.argsort(lookup)].reshape(leading, -1)


def translate(density, lists, operators):
    channels = density.shape[0]
    extent = density.shape[1:]
    padded = jnp.pad(density.astype(jnp.float32), ((0, 0), (3, 3), (3, 3), (3, 3)))
    running = jnp.zeros(density.shape, jnp.float32)
    for number, offset in enumerate(SHIFTS):
        targets = []
        sources = []
        for axis_number in range(3):
            start_at = 1 if offset[axis_number] == -3 else 0
            stride = 2 if abs(offset[axis_number]) == 3 else 1
            targets.append(slice(start_at, extent[axis_number], stride))
            sources.append(slice(3 + offset[axis_number] + start_at, 3 + offset[axis_number] + extent[axis_number], stride))
        present = (lists[number][targets[0], targets[1], targets[2]] >= 0).astype(jnp.float32)
        picked = padded[:, sources[0], sources[1], sources[2]] * present
        shape_now = picked.shape
        product = jnp.dot(operators[number].astype(jnp.float32), picked.reshape(channels, -1), precision=lax.Precision.HIGHEST)
        running = running.at[:, targets[0], targets[1], targets[2]].add(product.reshape(shape_now))
    return running


def reference(multipole, upward_maps, transfer_maps, downward_maps, check_inverse, fine_lists, coarse_lists):
    channels = multipole.shape[0]
    fine_brick = (BX, BY, BZ)
    coarse_brick = (BX // 2, BY // 2, BZ // 2)
    fine_grid = to_grid(multipole, fine_brick, N_CURVE)
    size_x, size_y, size_z = fine_grid.shape[1:]
    children = fine_grid.reshape(channels, size_x // 2, 2, size_y // 2, 2, size_z // 2, 2).transpose(2, 4, 6, 0, 1, 3, 5).reshape(8, channels, -1)
    parents = jnp.einsum("opq,oqc->pc", upward_maps.astype(jnp.float32), children.astype(jnp.float32), precision=lax.Precision.HIGHEST).astype(jnp.bfloat16)
    parent_grid = parents.reshape(channels, size_x // 2, size_y // 2, size_z // 2)
    coarse_check = 0.5 * translate(parent_grid, to_grid(coarse_lists, coarse_brick, N_CURVE), transfer_maps)
    coarse_local = coarse_check.astype(jnp.bfloat16).reshape(channels, -1)
    spread = jnp.einsum("opq,qc->opc", downward_maps.astype(jnp.float32), coarse_local.astype(jnp.float32), precision=lax.Precision.HIGHEST)
    spread = spread.reshape(2, 2, 2, channels, size_x // 2, size_y // 2, size_z // 2).transpose(3, 4, 0, 5, 1, 6, 2).reshape(channels, size_x, size_y, size_z)
    fine_check = translate(fine_grid, to_grid(fine_lists, fine_brick, N_CURVE), transfer_maps)
    fine_total = (fine_check + spread).astype(jnp.bfloat16)
    result = jnp.dot(check_inverse, fine_total.reshape(channels, -1), preferred_element_type=jnp.float32).astype(jnp.bfloat16)
    return from_grid(result.reshape(channels, size_x, size_y, size_z), fine_brick, N_CURVE)
```

```python
import functools

import jax
import jax.numpy as jnp
import numpy as np
from jax import lax
from jax.experimental import pallas as pl
from jax.experimental.pallas import tpu as pltpu
from jax.sharding import PartitionSpec as P

Q = 152
OFFS = 316
F32 = jnp.float32
BF16 = jnp.bfloat16
NN = (((1,), (0,)), ((), ()))
NT = (((1,), (1,)), ((), ()))
TN = (((0,), (0,)), ((), ()))
MESH = pl.DeviceIdType.MESH

SHIFTS = [
    (i, j, k)
    for i in range(-3, 4)
    for j in range(-3, 4)
    for k in range(-3, 4)
    if max(abs(i), abs(j), abs(k)) >= 2
]
NUMBER = {offset: number for number, offset in enumerate(SHIFTS)}
SIDES = [(i, j, k) for i in (-1, 0, 1) for j in (-1, 0, 1) for k in (-1, 0, 1)]
OCTANTS = [(a, b, c) for a in (0, 1) for b in (0, 1) for c in (0, 1)]


def piece_rows(side):
    ranges = []
    for component, extent in zip(side, (4, 4, 8)):
        ranges.append({-1: [extent - 1], 0: list(range(extent)), 1: [0]}[component])
    return [(x, y, z) for x in ranges[0] for y in ranges[1] for z in ranges[2]]


def piece_places():
    places, row = {}, 0
    order = [s for s in SIDES if s[0] == -1] + [(0, 0, 0)] + [s for s in SIDES if s[0] == 0 and s != (0, 0, 0)]
    order += [s for s in SIDES if s[0] == 1]
    for side in order:
        size = -(-len(piece_rows(side)) // 16) * 16
        places[side] = (row, size)
        row += size
    return places, row


PLACES, ROWS = piece_places()
OWN = PLACES[(0, 0, 0)][0]
SPAN = {-1: (0, OWN + 288), 0: (OWN, OWN + 288), 1: (OWN, ROWS)}


def send_picks():
    picks = np.zeros((ROWS, 128), np.float32)
    for side, (row, _) in PLACES.items():
        for number, (x, y, z) in enumerate(piece_rows(side)):
            picks[row + number, x * 32 + y * 8 + z] = 1
    return picks


def window_rows():
    rows = np.zeros((27, 128), np.int32)
    for number, shift in enumerate(SIDES):
        for x in range(4):
            for y in range(4):
                for z in range(8):
                    at = (x + shift[0], y + shift[1], z + shift[2])
                    side = tuple((-1 if c < 0 else 1 if c >= e else 0) for c, e in zip(at, (4, 4, 8)))
                    wrapped = tuple(c % e for c, e in zip(at, (4, 4, 8)))
                    rows[number, x * 32 + y * 8 + z] = PLACES[side][0] + piece_rows(side).index(wrapped)
    return rows


def coarse_window_picks():
    picks = np.zeros((27 * 16, 27 * 16), np.float32)
    for number, shift in enumerate(SIDES):
        for x in range(2):
            for y in range(2):
                for z in range(4):
                    at = (x + shift[0], y + shift[1], z + shift[2])
                    side = tuple((-1 if c < 0 else 1 if c >= e else 0) for c, e in zip(at, (2, 2, 4)))
                    wrapped = tuple(c % e for c, e in zip(at, (2, 2, 4)))
                    row = SIDES.index(side) * 16 + wrapped[0] * 8 + wrapped[1] * 4 + wrapped[2]
                    picks[number * 16 + x * 8 + y * 4 + z, row] = 1
    return picks


def fine_places():
    places = np.zeros((1, 1024), np.int32)
    for o, (a, b, c) in enumerate(OCTANTS):
        for x in range(4):
            for y in range(4):
                for z in range(8):
                    places[0, o * 128 + x * 32 + y * 8 + z] = ((2 * x + a) * 8 + 2 * y + b) * 16 + 2 * z + c
    return places


def coarse_picks():
    picks = np.zeros((128, 128), np.float32)
    for o, (a, b, c) in enumerate(OCTANTS):
        for x in range(2):
            for y in range(2):
                for z in range(4):
                    picks[o * 16 + x * 8 + y * 4 + z, ((2 * x + a) * 4 + 2 * y + b) * 8 + 2 * z + c] = 1
    return picks


def window_of(offset, octant):
    direction, source = [], []
    for d, a in zip(offset, octant):
        direction.append(min(1, max(-1, (a + d) // 2)))
        source.append((a + d) % 2)
    number = (direction[0] + 1) * 9 + (direction[1] + 1) * 3 + direction[2] + 1
    return number * 8 + source[0] * 4 + source[1] * 2 + source[2]


def kind(component):
    return 0 if abs(component) < 3 else component


def groups():
    by_kind = {}
    for offset in SHIFTS:
        by_kind.setdefault(tuple(kind(c) for c in offset), []).append(offset)

    def octants_of(kinds):
        return [o for o in OCTANTS if all(k == 0 or (k == 3) == (a == 0) for k, a in zip(kinds, o))]

    middle = by_kind[(0, 0, 0)]
    cuts = [[o for o in middle if o[0] == -2]]
    inner = [o for o in middle if abs(o[0]) < 2]
    cuts += [inner[:25], inner[25:] + [None, None], [o for o in middle if o[0] == 2]]
    eight = [(cut, OCTANTS) for cut in cuts]
    four, two = [], []
    for kinds, offsets in sorted(by_kind.items()):
        edges = sum(k != 0 for k in kinds)
        if edges == 1:
            four.append((offsets, octants_of(kinds)))
        if edges == 2:
            offsets = list(offsets)
            if kinds[2] == 0:
                offsets += by_kind[kinds[:2] + (-3,)] + by_kind[kinds[:2] + (3,)]
            two.append((offsets + [None] * (8 - len(offsets)), octants_of(kinds)))
    return eight, four, two


def table(members):
    slots, octants = [], []
    for offsets, octs in members:
        octants += [OCTANTS.index(o) for o in octs]
        for offset in offsets:
            if offset is None:
                slots += [NUMBER[offsets[0]], OFFS] + [window_of(offsets[0], o) for o in octs]
            else:
                slots += [NUMBER[offset], NUMBER[offset]] + [window_of(offset, o) for o in octs]
    return np.array(slots, np.int32), np.array(octants, np.int32)


EIGHT, FOUR, TWO = groups()
PLANES = [(min(n for n, o in enumerate(SHIFTS) if o[0] == d), sum(o[0] == d for o in SHIFTS)) for d in range(-3, 4)]
PLANE_ORDER = [1, 2, 3, 4, 5, 0, 6]


def neighbour(me, shift):
    def bit(place):
        return me // 2**place % 2

    x = (bit(2) + 2 * bit(5) + shift[0] + 4) % 4
    y = (bit(1) + 2 * bit(4) + shift[1] + 4) % 4
    z = (bit(0) + 2 * bit(3) + 4 * bit(6) + shift[2] + 8) % 8
    return (
        z % 2 + 2 * (y % 2) + 4 * (x % 2) + 8 * (z // 2 % 2) + 16 * (y // 2) + 32 * (x // 2) + 64 * (z // 4)
    )


def spread_lanes(blocks, copies=False):
    gap = jnp.zeros((blocks[0].shape[0], 8), blocks[0].dtype)
    return jnp.concatenate([part for block in blocks for part in (block, gap)], axis=1)


def exchange_kernel(mult, up, picks, cpicks, ef, ec, sent, csent, send, recv, csend, crecv):
    me = lax.axis_index("curve")
    others = [s for s in SIDES if s != (0, 0, 0)]
    barrier = pltpu.get_barrier_semaphore()
    for side in others:
        pl.semaphore_signal(barrier, inc=1, device_id=(neighbour(me, side),), device_id_type=MESH)

    row = lax.broadcasted_iota(jnp.int32, (128, 1), 0)
    base = row // 32 * 256 + row // 8 % 4 * 32 + row % 8 * 2
    lane = lax.broadcasted_iota(jnp.int32, (128, 1024), 1)
    rests, coarse = [], jnp.zeros((128, Q), F32)
    for o, (a, b, c) in enumerate(OCTANTS):
        pick = (lane == base + (a * 128 + b * 16 + c)).astype(F32).astype(BF16)
        child = lax.dot_general(pick, mult[...], NT, preferred_element_type=F32)
        ef[OWN : OWN + 128, o * 128 : (o + 1) * 128] = child[:, :128].astype(BF16)
        rests.append(child[:, 128:])
        coarse += lax.dot_general(child.astype(BF16), up[o], NT, preferred_element_type=F32)
    ef[OWN : OWN + 128, 1024:1280] = spread_lanes(rests).astype(BF16)
    sent[...] = lax.dot_general(
        picks[...], ef[OWN : OWN + 128, :], NN, preferred_element_type=F32
    ).astype(BF16)

    pl.semaphore_wait(barrier, 26)
    copies = []
    for number, side in enumerate(others):
        start, size = PLACES[side]
        to = neighbour(me, tuple(-c for c in side))
        copies.append(
            pltpu.make_async_remote_copy(
                src_ref=sent.at[pl.ds(start, size)],
                dst_ref=ef.at[pl.ds(start, size)],
                send_sem=send.at[number],
                recv_sem=recv.at[number],
                device_id=(to,),
                device_id_type=MESH,
            )
        )
        copies[-1].start()

    coarse = coarse.astype(BF16)
    rests = []
    mine = lax.dot_general(cpicks[...], coarse, NN, preferred_element_type=F32)
    for o in range(8):
        csent[:, o * 128 : (o + 1) * 128] = mine[o * 16 : (o + 1) * 16, :128].astype(BF16)
        rests.append(mine[o * 16 : (o + 1) * 16, 128:])
    csent[:, 1024:1280] = spread_lanes(rests).astype(BF16)
    for number, side in enumerate(others):
        to = neighbour(me, tuple(-c for c in side))
        copies.append(
            pltpu.make_async_remote_copy(
                src_ref=csent,
                dst_ref=ec.at[SIDES.index(side)],
                send_sem=csend.at[number],
                recv_sem=crecv.at[number],
                device_id=(to,),
                device_id_type=MESH,
            )
        )
        copies[-1].start()
    ec[13] = csent[...]
    for copy in copies:
        copy.wait()


def exchange(multipole, upward_maps):
    vmem = pl.BlockSpec(memory_space=pltpu.VMEM)
    return pl.pallas_call(
        exchange_kernel,
        out_shape=[
            jax.ShapeDtypeStruct((ROWS, 1280), BF16),
            jax.ShapeDtypeStruct((27, 16, 1280), BF16),
        ],
        in_specs=[vmem] * 4,
        out_specs=[vmem] * 2,
        scratch_shapes=[
            pltpu.VMEM((ROWS, 1280), BF16),
            pltpu.VMEM((16, 1280), BF16),
            pltpu.SemaphoreType.DMA((26,)),
            pltpu.SemaphoreType.DMA((26,)),
            pltpu.SemaphoreType.DMA((26,)),
            pltpu.SemaphoreType.DMA((26,)),
        ],
        compiler_params=pltpu.CompilerParams(
            collective_id=0, has_side_effects=True, vmem_limit_bytes=40 << 20
        ),
        name="exchange",
    )(multipole, upward_maps, jnp.asarray(send_picks(), BF16), jnp.asarray(coarse_picks(), BF16))


def translate_kernel(
    t8, o8, t4, o4, t2, o2, ef, ec, maps, fine_lists, coarse_lists, down, inverse,
    wrows, wcpicks, places, cpicks, out,
    mbuf, window, cmain, crest, mask, cmask, perm, lhs, rhs, crhs, acc, cacc, sems,
):
    loads = [
        pltpu.make_async_copy(maps.at[pl.ds(*PLANES[n])], mbuf.at[pl.ds(*PLANES[n])], sems.at[n])
        for n in range(7)
    ]
    for n in PLANE_ORDER:
        loads[n].start()

    for at in range(0, 1024, 128):
        box = lax.broadcasted_iota(jnp.int32, (128, 1024), 0) + at
        perm[at : at + 128, :] = (box == places[...]).astype(F32).astype(BF16)

    present = (fine_lists[...] >= 0).astype(F32).astype(BF16)
    for o in range(8):
        mask[o, 0:OFFS, :] = lax.dot_general(
            present, perm[:, o * 128 : (o + 1) * 128], NN, preferred_element_type=F32
        )
        mask[o, OFFS : OFFS + 4, :] = jnp.zeros((4, 128), F32)
    cmask[0:OFFS, :] = (coarse_lists[...] >= 0).astype(F32)
    cmask[OFFS : OFFS + 4, :] = jnp.zeros((4, 128), F32)

    for dx in (-1, 0, 1):
        first, last = SPAN[dx]
        iota = lax.broadcasted_iota(jnp.int32, (last - first, 1152), 0) + first
        pick = (iota == wrows[:, (dx + 1) * 1152 : (dx + 2) * 1152]).astype(F32).astype(BF16)

        def block(i, _, first=first, last=last, pick=pick, dx=dx):
            lanes = pl.ds(pl.multiple_of(i * 128, 128), 128)
            got = lax.dot_general(
                ef[first:last, lanes], pick, TN, preferred_element_type=F32
            ).astype(BF16)
            for n in range(9):
                window[((dx + 1) * 9 + n) * 8 + i, 0:128, :] = got[:, n * 128 : (n + 1) * 128]
            return 0

        lax.fori_loop(0, 8, block, 0)
        for half in range(2):
            got = lax.dot_general(
                ef[first:last, 1024 + half * 128 : 1152 + half * 128], pick, TN, preferred_element_type=F32
            ).astype(BF16)
            for n in range(9):
                for c in range(4):
                    window[((dx + 1) * 9 + n) * 8 + half * 4 + c, 128:160, :] = got[
                        c * 32 : (c + 1) * 32, n * 128 : (n + 1) * 128
                    ]

    source = ec[...].reshape(27 * 16, 1280)
    for c in range(8):
        got = lax.dot_general(
            wcpicks[...], source[:, c * 128 : (c + 1) * 128], NN, preferred_element_type=F32
        ).astype(BF16)
        rest = lax.dot_general(
            wcpicks[...], source[:, 1024 + c * 32 : 1056 + c * 32], NN, preferred_element_type=F32
        )
        rest = jnp.concatenate([rest] * 4, axis=1).astype(BF16)
        for n in range(27):
            cmain[n * 8 + c] = got[n * 16 : (n + 1) * 16]
            crest[n * 8 + c] = rest[n * 16 : (n + 1) * 16]

    acc[...] = jnp.zeros_like(acc)
    cacc[...] = jnp.zeros_like(cacc)
    group_of_lane = lax.broadcasted_iota(jnp.int32, (16, 128), 1) // 32

    def body(i, tab, octs, slots, n):
        width = -(-slots * 160 // 256) * 256
        rests = -(-slots // 4)
        at = [(i * slots + j) * (2 + n) for j in range(slots)]
        km = [tab[a] for a in at]
        kk = [tab[a + 1] for a in at]
        for j in range(slots):
            lhs[:, j * 128 : (j + 1) * 128] = mbuf[km[j], :, 0:128]
        for g in range(rests):
            parts = [mbuf[km[j], :, 128:Q].astype(F32) for j in range(4 * g, min(4 * g + 4, slots))]
            gap = jnp.zeros((Q, 8), F32)
            parts = [x for part in parts for x in (part, gap)]
            room = 128 - 32 * (len(parts) // 2)
            if room:
                parts.append(jnp.zeros((Q, room), F32))
            lhs[:, (slots + g) * 128 : (slots + g + 1) * 128] = jnp.concatenate(parts, axis=1).astype(BF16)
        if (slots + rests) * 128 < width:
            lhs[:, (slots + rests) * 128 : width] = jnp.zeros((Q, width - (slots + rests) * 128), BF16)
        for pair in range(n // 2):
            buffer = rhs[pair % 2]
            for half in range(2):
                o = octs[i * n + 2 * pair + half]
                cols = slice(half * 128, half * 128 + 128)
                for j in range(slots):
                    w = tab[at[j] + 2 + 2 * pair + half]
                    m = jnp.broadcast_to(mask[o, pl.ds(kk[j], 1), :], (16, 128)).astype(BF16)
                    m8 = jnp.concatenate([m] * 8, axis=0)
                    buffer[j * 128 : (j + 1) * 128, cols] = window[w, 0:128, :] * m8
                    rest_at = slots * 128 + j * 32
                    buffer[rest_at : rest_at + 32, cols] = window[w, 128:160, :] * m8[:32]
            if slots * 160 < width:
                buffer[slots * 160 : width, :] = jnp.zeros((width - slots * 160, 256), BF16)
            got = lax.dot_general(lhs[:, 0:width], buffer[0:width, :], NN, preferred_element_type=F32)
            for half in range(2):
                o = octs[i * n + 2 * pair + half]
                acc[o] += got[:, half * 128 : half * 128 + 128]
        rows = jnp.concatenate([cmask[pl.ds(kk[j], 1), :] for j in range(slots)], axis=0)
        chosen = jnp.concatenate([cpicks[octs[i * n + q]] for q in range(n)], axis=0)
        cm = lax.dot_general(chosen, rows.astype(BF16), NT, preferred_element_type=F32)
        for q in range(n):
            r = slice(q * 16, q * 16 + 16)
            for g in range(rests):
                total = None
                for j in range(4 * g, min(4 * g + 4, slots)):
                    w = tab[at[j] + 2 + q]
                    m = jnp.broadcast_to(cm[r, j : j + 1], (16, 128))
                    crhs[r, j * 128 : (j + 1) * 128] = cmain[w] * m.astype(BF16)
                    m = jnp.where(group_of_lane == j - 4 * g, m, 0.0).astype(BF16)
                    term = crest[w] * m
                    total = term if total is None else total + term
                crhs[r, (slots + g) * 128 : (slots + g + 1) * 128] = total
        if (slots + rests) * 128 < width:
            crhs[:, (slots + rests) * 128 : width] = jnp.zeros((128, width - (slots + rests) * 128), BF16)
        got = lax.dot_general(crhs[0 : n * 16, 0:width], lhs[:, 0:width], NT, preferred_element_type=F32)
        for q in range(n):
            cacc[octs[i * n + q]] += got[q * 16 : q * 16 + 16]

    def eight(i, _):
        for step, planes in enumerate(((1,), (2, 3), (4,), (5, 0, 6))):

            @pl.when(i == step)
            def _(planes=planes):
                for n in planes:
                    loads[n].wait()

        body(i, t8, o8, 25, 8)
        return 0

    lax.fori_loop(0, 4, eight, 0)

    def four(i, _):
        body(i, t4, o4, 25, 4)
        return 0

    lax.fori_loop(0, 6, four, 0)

    def two(i, _):
        body(i, t2, o2, 8, 2)
        return 0

    lax.fori_loop(0, 12, two, 0)

    local_rows = (0.5 * cacc[...].reshape(128, Q)).astype(BF16)
    picks = cpicks[...].reshape(128, 128)
    local = lax.dot_general(local_rows, picks, TN, preferred_element_type=F32).astype(BF16)
    for o in range(8):
        total = acc[o] + lax.dot_general(down[o], local, NN, preferred_element_type=F32)
        density = lax.dot_general(inverse[...], total.astype(BF16), NN, preferred_element_type=F32)
        lhs[:, o * 128 : (o + 1) * 128] = density.astype(BF16)
    out[...] = lax.dot_general(lhs[:, 0:1024], perm[...], NT, preferred_element_type=F32).astype(BF16)


def translate(ef, ec, maps, fine_lists, coarse_lists, down, inverse):
    vmem = pl.BlockSpec(memory_space=pltpu.VMEM)
    smem = pl.BlockSpec(memory_space=pltpu.SMEM)
    tables = [jnp.asarray(part) for members in (EIGHT, FOUR, TWO) for part in table(members)]
    return pl.pallas_call(
        translate_kernel,
        out_shape=jax.ShapeDtypeStruct((Q, 1024), BF16),
        in_specs=[smem] * 6 + [vmem] * 2 + [pl.BlockSpec(memory_space=pl.ANY)] + [vmem] * 8,
        out_specs=vmem,
        scratch_shapes=[
            pltpu.VMEM((OFFS, Q, Q), BF16),
            pltpu.VMEM((216, 160, 128), BF16),
            pltpu.VMEM((216, 16, 128), BF16),
            pltpu.VMEM((216, 16, 128), BF16),
            pltpu.VMEM((8, OFFS + 4, 128), F32),
            pltpu.VMEM((OFFS + 4, 128), F32),
            pltpu.VMEM((1024, 1024), BF16),
            pltpu.VMEM((Q, 4096), BF16),
            [pltpu.VMEM((4096, 256), BF16)] * 2,
            pltpu.VMEM((128, 4096), BF16),
            pltpu.VMEM((8, Q, 128), F32),
            pltpu.VMEM((8, 16, Q), F32),
            pltpu.SemaphoreType.DMA((7,)),
        ],
        compiler_params=pltpu.CompilerParams(vmem_limit_bytes=62 << 20),
        name="translate",
    )(
        *tables, ef, ec, maps, fine_lists, coarse_lists, down, inverse,
        jnp.asarray(window_rows().reshape(1, -1)), jnp.asarray(coarse_window_picks(), BF16),
        jnp.asarray(fine_places()), jnp.asarray(coarse_picks().reshape(8, 16, 128), BF16),
    )


def local(multipole, upward_maps, transfer_maps, downward_maps, check_inverse, fine_lists, coarse_lists):
    ef, ec = exchange(multipole, upward_maps)
    return translate(ef, ec, transfer_maps, fine_lists, coarse_lists, downward_maps, check_inverse)


def solution(mesh):
    placed = (P(None, "curve"), P(), P(), P(), P(), P(None, "curve"), P(None, "curve"))
    return jax.shard_map(local, mesh=mesh, in_specs=placed, out_specs=P(None, "curve"), check_vma=False)
```

```python
import functools

import jax
import jax.numpy as jnp
import numpy as np
from jax import lax
from jax.experimental import pallas as pl
from jax.experimental.pallas import tpu as pltpu
from jax.sharding import PartitionSpec as P

Q = 152
OFFS = 316
F32 = jnp.float32
BF16 = jnp.bfloat16
PAIR, DEEP = 2, 1024
NN = (((1,), (0,)), ((), ()))
NT = (((1,), (1,)), ((), ()))
TN = (((0,), (0,)), ((), ()))
MESH = pl.DeviceIdType.MESH

SHIFTS = [
    (i, j, k)
    for i in range(-3, 4)
    for j in range(-3, 4)
    for k in range(-3, 4)
    if max(abs(i), abs(j), abs(k)) >= 2
]
NUMBER = {offset: number for number, offset in enumerate(SHIFTS)}
SIDES = [(i, j, k) for i in (-1, 0, 1) for j in (-1, 0, 1) for k in (-1, 0, 1)]
OCTANTS = [(a, b, c) for a in (0, 1) for b in (0, 1) for c in (0, 1)]


FINE = (4, 4, 8)
COARSE = (2, 2, 4)


def piece_rows(side, extents=FINE):
    ranges = []
    for component, extent in zip(side, extents):
        ranges.append({-1: [extent - 1], 0: list(range(extent)), 1: [0]}[component])
    return [(x, y, z) for x in ranges[0] for y in ranges[1] for z in ranges[2]]


def folding(count):
    tiles = {8: 5, 4: 3, 2: 2, 1: 1}.get(count, 10)
    return tiles, -(-10 // tiles)


def piece_places():
    places, row = {}, 0
    order = [s for s in SIDES if s[0] == -1] + [(0, 0, 0)] + [s for s in SIDES if s[0] == 0 and s != (0, 0, 0)]
    order += [s for s in SIDES if s[0] == 1]
    for side in order:
        size = -(-len(piece_rows(side)) // 16) * 16
        places[side] = (row, size)
        row += size
    return places, row


PLACES, ROWS = piece_places()
OWN = PLACES[(0, 0, 0)][0]
SPAN = {-1: (0, OWN + 288), 0: (OWN, OWN + 288), 1: (OWN, ROWS)}


def piece_picks(side, extents, size):
    picks = np.zeros((size, extents[0] * extents[1] * extents[2]), np.float32)
    rows = piece_rows(side, extents)
    for fold in range(folding(len(rows))[1]):
        for number, (x, y, z) in enumerate(rows):
            picks[fold * len(rows) + number, (x * extents[1] + y) * extents[2] + z] = 1
    return picks


def send_picks():
    picks = np.zeros((ROWS, 128), np.float32)
    for side, (row, size) in PLACES.items():
        picks[row : row + size] = piece_picks(side, FINE, size)
    return picks


def coarse_send_picks():
    return np.concatenate([piece_picks(side, COARSE, 16) for side in SIDES])


def window_rows():
    rows = np.zeros((27, 128), np.int32)
    for number, shift in enumerate(SIDES):
        for x in range(4):
            for y in range(4):
                for z in range(8):
                    at = (x + shift[0], y + shift[1], z + shift[2])
                    side = tuple((-1 if c < 0 else 1 if c >= e else 0) for c, e in zip(at, (4, 4, 8)))
                    wrapped = tuple(c % e for c, e in zip(at, (4, 4, 8)))
                    rows[number, x * 32 + y * 8 + z] = PLACES[side][0] + piece_rows(side).index(wrapped)
    return rows


def coarse_window_picks():
    picks = np.zeros((27 * 16, 27 * 16), np.float32)
    for number, shift in enumerate(SIDES):
        for x in range(2):
            for y in range(2):
                for z in range(4):
                    at = (x + shift[0], y + shift[1], z + shift[2])
                    side = tuple((-1 if c < 0 else 1 if c >= e else 0) for c, e in zip(at, (2, 2, 4)))
                    wrapped = tuple(c % e for c, e in zip(at, (2, 2, 4)))
                    row = SIDES.index(side) * 16 + piece_rows(side, COARSE).index(wrapped)
                    picks[number * 16 + x * 8 + y * 4 + z, row] = 1
    return picks


def fine_places():
    places = np.zeros((1, 1024), np.int32)
    for o, (a, b, c) in enumerate(OCTANTS):
        for x in range(4):
            for y in range(4):
                for z in range(8):
                    places[0, o * 128 + x * 32 + y * 8 + z] = ((2 * x + a) * 8 + 2 * y + b) * 16 + 2 * z + c
    return places


def coarse_picks():
    picks = np.zeros((128, 128), np.float32)
    for o, (a, b, c) in enumerate(OCTANTS):
        for x in range(2):
            for y in range(2):
                for z in range(4):
                    picks[o * 16 + x * 8 + y * 4 + z, ((2 * x + a) * 4 + 2 * y + b) * 8 + 2 * z + c] = 1
    return picks


def window_of(offset, octant):
    direction, source = [], []
    for d, a in zip(offset, octant):
        direction.append(min(1, max(-1, (a + d) // 2)))
        source.append((a + d) % 2)
    number = (direction[0] + 1) * 9 + (direction[1] + 1) * 3 + direction[2] + 1
    return number * 8 + source[0] * 4 + source[1] * 2 + source[2]


def kind(component):
    return 0 if abs(component) < 3 else component


def groups():
    by_kind = {}
    for offset in SHIFTS:
        by_kind.setdefault(tuple(kind(c) for c in offset), []).append(offset)

    def octants_of(kinds):
        return [o for o in OCTANTS if all(k == 0 or (k == 3) == (a == 0) for k, a in zip(kinds, o))]

    middle = by_kind[(0, 0, 0)]
    cuts = [[o for o in middle if o[0] == -2]]
    inner = [o for o in middle if abs(o[0]) < 2]
    cuts += [inner[:25], inner[25:] + [None, None], [o for o in middle if o[0] == 2]]
    eight = [(cut, OCTANTS) for cut in cuts]
    four, two = [], []
    for kinds, offsets in sorted(by_kind.items()):
        edges = sum(k != 0 for k in kinds)
        if edges == 1:
            four.append((offsets, octants_of(kinds)))
        if edges == 2:
            offsets = list(offsets)
            if kinds[2] == 0:
                offsets += by_kind[kinds[:2] + (-3,)] + by_kind[kinds[:2] + (3,)]
            two.append((offsets + [None] * (8 - len(offsets)), octants_of(kinds)))
    return eight, four, two


def table(members):
    slots, octants = [], []
    for offsets, octs in members:
        octants += [OCTANTS.index(o) for o in octs]
        for offset in offsets:
            if offset is None:
                slots += [NUMBER[offsets[0]], OFFS] + [window_of(offsets[0], o) for o in octs]
            else:
                slots += [NUMBER[offset], NUMBER[offset]] + [window_of(offset, o) for o in octs]
    return np.array(slots, np.int32), np.array(octants, np.int32)


EIGHT, FOUR, TWO = groups()


PLANES = [(min(n for n, o in enumerate(SHIFTS) if o[0] == d), sum(o[0] == d for o in SHIFTS)) for d in range(-3, 4)]
PLANE_ORDER = [1, 2, 3, 4, 5, 0, 6]


def brick_of(me):
    def bit(place):
        return me // 2**place % 2

    return bit(2) + 2 * bit(5), bit(1) + 2 * bit(4), bit(0) + 2 * bit(3) + 4 * bit(6)


def neighbour(me, shift):
    x, y, z = [(c + d + e) % e for c, d, e in zip(brick_of(me), shift, (4, 4, 8))]
    return (
        z % 2 + 2 * (y % 2) + 4 * (x % 2) + 8 * (z // 2 % 2) + 16 * (y // 2) + 32 * (x // 2) + 64 * (z // 4)
    )


def inside(me, shift):
    found = True
    for c, d, e in zip(brick_of(me), shift, (4, 4, 8)):
        if d == 1:
            found = jnp.logical_and(found, c < e - 1)
        if d == -1:
            found = jnp.logical_and(found, c > 0)
    return found


def fold(piece, count):
    tiles, folds = folding(count)
    row = lax.broadcasted_iota(jnp.int32, (16, tiles * 128), 0) // count
    total = jnp.zeros((16, tiles * 128), F32)
    for number in range(folds):
        part = piece[:, number * tiles * 128 : min((number + 1) * tiles, 10) * 128]
        if part.shape[1] < tiles * 128:
            part = jnp.concatenate([part, jnp.zeros((16, tiles * 128 - part.shape[1]), F32)], axis=1)
        total = jnp.where(row == number, part, total)
    return total.astype(BF16)


def unfold(piece, count):
    folds = folding(count)[1]
    piece = piece.astype(F32)
    flat = jnp.concatenate([piece[k * count : (k + 1) * count] for k in range(folds)], axis=1)[:, :1280]
    return jnp.concatenate([flat, jnp.zeros((16 - count, 1280), F32)], axis=0).astype(BF16)


def spread_lanes(blocks, copies=False):
    gap = jnp.zeros((blocks[0].shape[0], 8), blocks[0].dtype)
    return jnp.concatenate([part for block in blocks for part in (block, gap)], axis=1)


def exchange_kernel(
    mult, up, picks, cpicks, cends, maps, ef, ec, heads, tails,
    sent, csent, slab, turned, turned_tail, head, tail, send, recv, csend, crecv, slab_sem, out_sem,
):
    me = lax.axis_index("curve")

    def fetch(i, size=16):
        return pltpu.make_async_copy(
            maps.at[pl.ds(i * 16, size)], slab.at[i % 2, pl.ds(0, size)], slab_sem.at[i % 2]
        )

    fetch(0).start()
    others = [s for s in SIDES if s != (0, 0, 0)]
    barrier = pltpu.get_barrier_semaphore()
    for side in others:
        pl.semaphore_signal(barrier, inc=1, device_id=(neighbour(me, side),), device_id_type=MESH)

    row = lax.broadcasted_iota(jnp.int32, (128, 1), 0)
    base = row // 32 * 256 + row // 8 % 4 * 32 + row % 8 * 2
    lane = lax.broadcasted_iota(jnp.int32, (128, 1024), 1)
    rests, coarse = [], jnp.zeros((128, Q), F32)
    for o, (a, b, c) in enumerate(OCTANTS):
        pick = (lane == base + (a * 128 + b * 16 + c)).astype(F32).astype(BF16)
        child = lax.dot_general(pick, mult[...], NT, preferred_element_type=F32)
        ef[OWN : OWN + 128, o * 128 : (o + 1) * 128] = child[:, :128].astype(BF16)
        rests.append(child[:, 128:])
        coarse += lax.dot_general(child.astype(BF16), up[o], NT, preferred_element_type=F32)
    ef[OWN : OWN + 128, 1024:1280] = spread_lanes(rests).astype(BF16)
    folded = [side for side in others if PLACES[side][1] == 16 and len(piece_rows(side)) < 16]
    for side in others:
        start, size = PLACES[side]
        count = len(piece_rows(side))
        piece = lax.dot_general(
            picks[start : start + size, :], ef[OWN : OWN + 128, :], NN, preferred_element_type=F32
        )
        tiles = folding(count)[0]
        sent[start : start + size, 0 : tiles * 128] = fold(piece, count) if side in folded else piece.astype(BF16)

        @pl.when(jnp.logical_not(inside(me, side)))
        def _(start=start, size=size, side=side):
            ef[start : start + size, :] = jnp.zeros((size, 1280), BF16)
            ec[SIDES.index(side)] = jnp.zeros((16, 1280), BF16)

    pl.semaphore_wait(barrier, 26)

    def fine_copy(number):
        side = others[number]
        start, size = PLACES[side]
        lanes = pl.ds(0, folding(len(piece_rows(side)))[0] * 128)
        return pltpu.make_async_remote_copy(
            src_ref=sent.at[pl.ds(start, size), lanes],
            dst_ref=ef.at[pl.ds(start, size), lanes],
            send_sem=send.at[number],
            recv_sem=recv.at[number],
            device_id=(neighbour(me, tuple(-c for c in side)),),
            device_id_type=MESH,
        )

    def coarse_copy(number):
        side = others[number]
        lanes = pl.ds(0, folding(len(piece_rows(side, COARSE)))[0] * 128)
        return pltpu.make_async_remote_copy(
            src_ref=csent.at[SIDES.index(side), :, lanes],
            dst_ref=ec.at[SIDES.index(side), :, lanes],
            send_sem=csend.at[number],
            recv_sem=crecv.at[number],
            device_id=(neighbour(me, tuple(-c for c in side)),),
            device_id_type=MESH,
        )

    def start_all(copy):
        for number, side in enumerate(others):

            @pl.when(inside(me, tuple(-c for c in side)))
            def _(number=number):
                copy(number).start()

    start_all(fine_copy)
    coarse = coarse.astype(BF16)
    rests = []
    mine = lax.dot_general(cpicks[...], coarse, NN, preferred_element_type=F32)
    for o in range(8):
        ec[13, :, o * 128 : (o + 1) * 128] = mine[o * 16 : (o + 1) * 16, :128].astype(BF16)
        rests.append(mine[o * 16 : (o + 1) * 16, 128:])
    ec[13, :, 1024:1280] = spread_lanes(rests).astype(BF16)
    for side in others:
        place, count = SIDES.index(side), len(piece_rows(side, COARSE))
        piece = lax.dot_general(
            cends[place * 16 : place * 16 + 16, :], ec[13], NN, preferred_element_type=F32
        )
        csent[place, :, 0 : folding(count)[0] * 128] = fold(piece, count)
    start_all(coarse_copy)

    def leave(i):
        rows = pl.ds(pl.multiple_of(i * 16, 16), 16)
        return [
            pltpu.make_async_copy(head.at[i % 2], heads.at[:, rows], out_sem.at[0, i % 2]),
            pltpu.make_async_copy(tail.at[i % 2], tails.at[:, rows], out_sem.at[1, i % 2]),
        ]

    def turn(i):
        def one(p, _):
            flat = jnp.swapaxes(slab[i % 2, p].astype(F32), 0, 1)
            turned[p, 0:OFFS, :] = flat[:, :128]
            turned_tail[p, 0:OFFS, 0 : Q - 128] = flat[:, 128:]
            return 0

        lax.fori_loop(0, 16, one, 0, unroll=4)

        def eight(k, _):
            at = pl.ds(pl.multiple_of(k * 8, 8), 8)
            head[i % 2, at] = jnp.swapaxes(turned[:, at, :], 0, 1).astype(BF16)
            tail[i % 2, at] = jnp.swapaxes(turned_tail[:, at, :], 0, 1).astype(BF16)
            return 0

        lax.fori_loop(0, 40, eight, 0, unroll=5)
        for part in leave(i):
            part.start()

    def step(i, _):
        fetch(i).wait()

        @pl.when(i < 8)
        def _():
            fetch(i + 1).start()

        @pl.when(i == 8)
        def _():
            fetch(9, 8).start()

        @pl.when(i >= 2)
        def _():
            for part in leave(i - 2):
                part.wait()

        turn(i)
        return 0

    lax.fori_loop(0, 9, step, 0)
    fetch(9, 8).wait()
    for part in leave(7):
        part.wait()
    turn(9)
    for copy in (fine_copy, coarse_copy):
        for number, side in enumerate(others):

            @pl.when(inside(me, tuple(-c for c in side)))
            def _(copy=copy, number=number):
                copy(number).wait_send()

            @pl.when(inside(me, side))
            def _(copy=copy, number=number):
                copy(number).wait_recv()

    for side in folded:
        rows, count = slice(PLACES[side][0], PLACES[side][0] + 16), len(piece_rows(side))
        ef[rows, :] = unfold(ef[rows, 0 : folding(count)[0] * 128], count)
    for side in others:
        place, count = SIDES.index(side), len(piece_rows(side, COARSE))
        ec[place] = unfold(ec[place, :, 0 : folding(count)[0] * 128], count)
    for part in leave(8) + leave(9):
        part.wait()


def exchange(multipole, upward_maps, maps):
    vmem = pl.BlockSpec(memory_space=pltpu.VMEM)
    return pl.pallas_call(
        exchange_kernel,
        out_shape=[
            jax.ShapeDtypeStruct((ROWS, 1280), BF16),
            jax.ShapeDtypeStruct((27, 16, 1280), BF16),
            jax.ShapeDtypeStruct((OFFS + 4, 160, 128), BF16),
            jax.ShapeDtypeStruct((OFFS + 4, 160, 128), BF16),
        ],
        in_specs=[vmem] * 5 + [pl.BlockSpec(memory_space=pl.ANY)],
        out_specs=[vmem] * 2 + [pl.BlockSpec(memory_space=pl.ANY)] * 2,
        scratch_shapes=[
            pltpu.VMEM((ROWS, 1280), BF16),
            pltpu.VMEM((27, 16, 640), BF16),
            pltpu.VMEM((2, 16, Q, OFFS), BF16),
            pltpu.VMEM((16, OFFS + 4, 128), F32),
            pltpu.VMEM((16, OFFS + 4, 128), F32),
            pltpu.VMEM((2, OFFS + 4, 16, 128), BF16),
            pltpu.VMEM((2, OFFS + 4, 16, 128), BF16),
            pltpu.SemaphoreType.DMA((26,)),
            pltpu.SemaphoreType.DMA((26,)),
            pltpu.SemaphoreType.DMA((26,)),
            pltpu.SemaphoreType.DMA((26,)),
            pltpu.SemaphoreType.DMA((2,)),
            pltpu.SemaphoreType.DMA((2, 2)),
        ],
        compiler_params=pltpu.CompilerParams(
            collective_id=0, has_side_effects=True, vmem_limit_bytes=40 << 20
        ),
        name="exchange",
    )(
        multipole, upward_maps, jnp.asarray(send_picks(), BF16), jnp.asarray(coarse_picks(), BF16),
        jnp.asarray(coarse_send_picks(), BF16), jnp.transpose(maps, (1, 2, 0)),
    )


def translate_kernel(
    t8, o8, t4, o4, t2, o2, ef, ec, heads_in, tails_in, fine_lists, coarse_lists, down, inverse,
    wrows, wcpicks, places, cpicks, out,
    heads, tails, pick, window, cmain, crest, mask, cmask, perm, lhs, crhs, acc, cacc, sems,
):
    loads = [
        [
            pltpu.make_async_copy(heads_in.at[pl.ds(*PLANES[n])], heads.at[pl.ds(*PLANES[n])], sems.at[0, n]),
            pltpu.make_async_copy(tails_in.at[pl.ds(*PLANES[n])], tails.at[pl.ds(*PLANES[n])], sems.at[1, n]),
        ]
        for n in range(7)
    ]
    for n in PLANE_ORDER:
        for part in loads[n]:
            part.start()

    for at in range(0, 1024, 128):
        box = lax.broadcasted_iota(jnp.int32, (128, 1024), 0) + at
        perm[at : at + 128, :] = (box == places[...]).astype(F32).astype(BF16)

    present = (fine_lists[...] >= 0).astype(F32).astype(BF16)
    for o in range(8):
        mask[o, 0:OFFS, :] = lax.dot_general(
            present, perm[:, o * 128 : (o + 1) * 128], NN, preferred_element_type=F32
        )
        mask[o, OFFS : OFFS + 4, :] = jnp.zeros((4, 128), F32)
    cmask[0:OFFS, :] = (coarse_lists[...] >= 0).astype(F32)
    cmask[OFFS : OFFS + 4, :] = jnp.zeros((4, 128), F32)

    for dx in (-1, 0, 1):
        first, last = SPAN[dx]
        span = last - first

        def mark(i, _, first=first, dx=dx):
            iota = lax.broadcasted_iota(jnp.int32, (16, 1152), 0) + (first + i * 16)
            wanted = wrows[:, (dx + 1) * 1152 : (dx + 2) * 1152]
            at = pl.ds(pl.multiple_of(i * 16, 16), 16)
            pick[at, :] = (iota == wanted).astype(F32).astype(BF16)
            return 0

        lax.fori_loop(0, span // 16, mark, 0)

        def block(i, _, first=first, last=last, span=span, dx=dx):
            lanes = pl.ds(pl.multiple_of(i * 128, 128), 128)
            got = lax.dot_general(
                ef[first:last, lanes], pick[0:span, :], TN, preferred_element_type=F32
            ).astype(BF16)
            for n in range(9):
                window[((dx + 1) * 9 + n) * 8 + i, 0:128, :] = got[:, n * 128 : (n + 1) * 128]
            return 0

        lax.fori_loop(0, 8, block, 0)
        for half in range(2):
            got = lax.dot_general(
                ef[first:last, 1024 + half * 128 : 1152 + half * 128], pick[0:span, :], TN, preferred_element_type=F32
            ).astype(BF16)
            for n in range(9):
                for c in range(4):
                    window[((dx + 1) * 9 + n) * 8 + half * 4 + c, 128:160, :] = got[
                        c * 32 : (c + 1) * 32, n * 128 : (n + 1) * 128
                    ]

    source = ec[...].reshape(27 * 16, 1280)
    for c in range(8):
        got = lax.dot_general(
            wcpicks[...], source[:, c * 128 : (c + 1) * 128], NN, preferred_element_type=F32
        ).astype(BF16)
        rest = lax.dot_general(
            wcpicks[...], source[:, 1024 + c * 32 : 1056 + c * 32], NN, preferred_element_type=F32
        )
        rest = jnp.concatenate([rest] * 4, axis=1).astype(BF16)
        group_of_lane = lax.broadcasted_iota(jnp.int32, (16, 128), 1) // 32
        for n in range(27):
            cmain[n * 8 + c] = got[n * 16 : (n + 1) * 16]
            for j in range(4):
                only = (group_of_lane == j).astype(F32).astype(BF16)
                crest[j, n * 8 + c] = rest[n * 16 : (n + 1) * 16] * only

    acc[...] = jnp.zeros_like(acc)
    cacc[...] = jnp.zeros_like(cacc)
    def body(i, tab, octs, slots, n):
        rests = -(-slots // 4)
        cut = slots // 2 + 1 if slots > 8 else slots
        kept = 16 - cut if slots > 8 else rests
        order = [("head", j) for j in range(cut)] + [("tail", g) for g in range(kept)]
        order += [("head", j) for j in range(cut, slots)] + [("tail", g) for g in range(kept, rests)]
        place = {block: number for number, block in enumerate(order)}
        width = len(order) * 128
        at = [(i * slots + j) * (2 + n) for j in range(slots)]
        km = [tab[a] for a in at]
        kk = [tab[a + 1] for a in at]
        members = [range(4 * g, min(4 * g + 4, slots)) for g in range(rests)]

        def span(kind, number):
            return slice(place[kind, number] * 128, place[kind, number] * 128 + 128)

        for j in range(slots):
            lhs[:, span("head", j)] = heads[km[j], 0:Q, :]
        for g in range(rests):
            parts = [tails[km[j], 0:Q, 0 : Q - 128].astype(F32) for j in members[g]]
            gap = jnp.zeros((Q, 8), F32)
            parts = [x for part in parts for x in (part, gap)]
            room = 128 - 32 * (len(parts) // 2)
            if room:
                parts.append(jnp.zeros((Q, room), F32))
            lhs[:, span("tail", g)] = jnp.concatenate(parts, axis=1).astype(BF16)

        def shown(q, blocks):
            o = octs[i * n + q]
            parts = []
            for kind, number in blocks:
                for j in [number] if kind == "head" else members[number]:
                    w = tab[at[j] + 2 + q]
                    m = jnp.broadcast_to(mask[o, pl.ds(kk[j], 1), :], (16, 128)).astype(BF16)
                    if kind == "head":
                        parts.append(window[w, 0:128, :] * jnp.concatenate([m] * 8, axis=0))
                    else:
                        parts.append(window[w, 128:160, :] * jnp.concatenate([m] * 2, axis=0))
                if kind == "tail" and len(members[number]) < 4:
                    parts.append(jnp.zeros((128 - 32 * len(members[number]), 128), BF16))
            return jnp.concatenate(parts, axis=0)

        for q in range(0, n, PAIR):
            got = None
            for first in range(0, width, DEEP):
                last = min(first + DEEP, width)
                blocks = order[first // 128 : last // 128]
                masked = jnp.concatenate([shown(q + h, blocks) for h in range(PAIR)], axis=1)
                term = lax.dot_general(lhs[:, first:last], masked, NN, preferred_element_type=F32)
                got = term if got is None else got + term
            for h in range(PAIR):
                acc[octs[i * n + q + h]] += got[:, h * 128 : h * 128 + 128]

        rows = jnp.concatenate([cmask[pl.ds(kk[j], 1), :] for j in range(slots)], axis=0)
        chosen = jnp.concatenate([cpicks[octs[i * n + q]] for q in range(n)], axis=0)
        cm = lax.dot_general(chosen, rows.astype(BF16), NT, preferred_element_type=F32)
        for q in range(n):
            r = slice(q * 16, q * 16 + 16)
            for g in range(rests):
                total = None
                for j in members[g]:
                    w = tab[at[j] + 2 + q]
                    m = jnp.broadcast_to(cm[r, j : j + 1], (16, 128)).astype(BF16)
                    crhs[r, span("head", j)] = cmain[w] * m
                    term = crest[j % 4, w] * m
                    total = term if total is None else total + term
                crhs[r, span("tail", g)] = total
        got = lax.dot_general(crhs[0 : n * 16, 0:width], lhs[:, 0:width], NT, preferred_element_type=F32)
        for q in range(n):
            cacc[octs[i * n + q]] += got[q * 16 : q * 16 + 16]

    def eight(i, _):
        for step, planes in enumerate(((1,), (2, 3), (4,), (5, 0, 6))):

            @pl.when(i == step)
            def _(planes=planes):
                for n in planes:
                    for part in loads[n]:
                        part.wait()

        body(i, t8, o8, 25, 8)
        return 0

    lax.fori_loop(0, 4, eight, 0)

    def four(i, _):
        body(i, t4, o4, 25, 4)
        return 0

    lax.fori_loop(0, 6, four, 0)

    def two(i, _):
        body(i, t2, o2, 8, 2)
        return 0

    lax.fori_loop(0, 12, two, 0)

    local_rows = (0.5 * cacc[...].reshape(128, Q)).astype(BF16)
    picks = cpicks[...].reshape(128, 128)
    local = lax.dot_general(local_rows, picks, TN, preferred_element_type=F32).astype(BF16)
    for o in range(8):
        total = acc[o] + lax.dot_general(down[o], local, NN, preferred_element_type=F32)
        density = lax.dot_general(inverse[...], total.astype(BF16), NN, preferred_element_type=F32)
        lhs[:, o * 128 : (o + 1) * 128] = density.astype(BF16)
    out[...] = lax.dot_general(lhs[:, 0:1024], perm[...], NT, preferred_element_type=F32).astype(BF16)


def translate(ef, ec, heads, tails, fine_lists, coarse_lists, down, inverse):
    vmem = pl.BlockSpec(memory_space=pltpu.VMEM)
    smem = pl.BlockSpec(memory_space=pltpu.SMEM)
    tables = [jnp.asarray(part) for members in (EIGHT, FOUR, TWO) for part in table(members)]
    return pl.pallas_call(
        translate_kernel,
        out_shape=jax.ShapeDtypeStruct((Q, 1024), BF16),
        in_specs=[smem] * 6 + [vmem] * 2 + [pl.BlockSpec(memory_space=pl.ANY)] * 2 + [vmem] * 8,
        out_specs=vmem,
        scratch_shapes=[
            pltpu.VMEM((OFFS + 4, 160, 128), BF16),
            pltpu.VMEM((OFFS + 4, 160, 128), BF16),
            pltpu.VMEM((448, 1152), BF16),
            pltpu.VMEM((216, 160, 128), BF16),
            pltpu.VMEM((216, 16, 128), BF16),
            pltpu.VMEM((4, 216, 16, 128), BF16),
            pltpu.VMEM((8, OFFS + 4, 128), F32),
            pltpu.VMEM((OFFS + 4, 128), F32),
            pltpu.VMEM((1024, 1024), BF16),
            pltpu.VMEM((Q, 4096), BF16),
            pltpu.VMEM((128, 4096), BF16),
            pltpu.VMEM((8, Q, 128), F32),
            pltpu.VMEM((8, 16, Q), F32),
            pltpu.SemaphoreType.DMA((2, 7)),
        ],
        compiler_params=pltpu.CompilerParams(vmem_limit_bytes=62 << 20),
        name="translate",
    )(
        *tables, ef, ec, heads, tails, fine_lists, coarse_lists, down, inverse,
        jnp.asarray(window_rows().reshape(1, -1)), jnp.asarray(coarse_window_picks(), BF16),
        jnp.asarray(fine_places()), jnp.asarray(coarse_picks().reshape(8, 16, 128), BF16),
    )


def local(multipole, upward_maps, transfer_maps, downward_maps, check_inverse, fine_lists, coarse_lists):
    ef, ec, heads, tails = exchange(multipole, upward_maps, transfer_maps)
    return translate(ef, ec, heads, tails, fine_lists, coarse_lists, downward_maps, check_inverse)


def solution(mesh):
    placed = (P(None, "curve"), P(), P(), P(), P(), P(None, "curve"), P(None, "curve"))
    return jax.shard_map(local, mesh=mesh, in_specs=placed, out_specs=P(None, "curve"), check_vma=False)
```

```python
import functools

import jax
import jax.numpy as jnp
import numpy as np
from jax import lax
from jax.experimental import pallas as pl
from jax.experimental.pallas import tpu as pltpu
from jax.sharding import PartitionSpec as P

Q = 152
OFFS = 316
F32 = jnp.float32
BF16 = jnp.bfloat16
PAIR, DEEP = 2, 1024
NN = (((1,), (0,)), ((), ()))
NT = (((1,), (1,)), ((), ()))
TN = (((0,), (0,)), ((), ()))
MESH = pl.DeviceIdType.MESH

SHIFTS = [
    (i, j, k)
    for i in range(-3, 4)
    for j in range(-3, 4)
    for k in range(-3, 4)
    if max(abs(i), abs(j), abs(k)) >= 2
]
NUMBER = {offset: number for number, offset in enumerate(SHIFTS)}
SIDES = [(i, j, k) for i in (-1, 0, 1) for j in (-1, 0, 1) for k in (-1, 0, 1)]
OCTANTS = [(a, b, c) for a in (0, 1) for b in (0, 1) for c in (0, 1)]


FINE = (4, 4, 8)
COARSE = (2, 2, 4)


def piece_rows(side, extents=FINE):
    ranges = []
    for component, extent in zip(side, extents):
        ranges.append({-1: [extent - 1], 0: list(range(extent)), 1: [0]}[component])
    return [(x, y, z) for x in ranges[0] for y in ranges[1] for z in ranges[2]]


def folding(count):
    tiles = {8: 5, 4: 3, 2: 2, 1: 1}.get(count, 10)
    return tiles, -(-10 // tiles)


def piece_places():
    places, row = {}, 0
    order = [s for s in SIDES if s[0] == -1] + [(0, 0, 0)] + [s for s in SIDES if s[0] == 0 and s != (0, 0, 0)]
    order += [s for s in SIDES if s[0] == 1]
    for side in order:
        size = -(-len(piece_rows(side)) // 16) * 16
        places[side] = (row, size)
        row += size
    return places, row


PLACES, ROWS = piece_places()
OWN = PLACES[(0, 0, 0)][0]
SPAN = {-1: (0, OWN + 288), 0: (OWN, OWN + 288), 1: (OWN, ROWS)}


def piece_picks(side, extents, size):
    picks = np.zeros((size, extents[0] * extents[1] * extents[2]), np.float32)
    rows = piece_rows(side, extents)
    for fold in range(folding(len(rows))[1]):
        for number, (x, y, z) in enumerate(rows):
            picks[fold * len(rows) + number, (x * extents[1] + y) * extents[2] + z] = 1
    return picks


def send_picks():
    picks = np.zeros((ROWS, 128), np.float32)
    for side, (row, size) in PLACES.items():
        picks[row : row + size] = piece_picks(side, FINE, size)
    return picks


def coarse_send_picks():
    return np.concatenate([piece_picks(side, COARSE, 16) for side in SIDES])


def window_rows():
    rows = np.zeros((27, 128), np.int32)
    for number, shift in enumerate(SIDES):
        for x in range(4):
            for y in range(4):
                for z in range(8):
                    at = (x + shift[0], y + shift[1], z + shift[2])
                    side = tuple((-1 if c < 0 else 1 if c >= e else 0) for c, e in zip(at, (4, 4, 8)))
                    wrapped = tuple(c % e for c, e in zip(at, (4, 4, 8)))
                    rows[number, x * 32 + y * 8 + z] = PLACES[side][0] + piece_rows(side).index(wrapped)
    return rows


def coarse_window_picks():
    picks = np.zeros((27 * 16, 27 * 16), np.float32)
    for number, shift in enumerate(SIDES):
        for x in range(2):
            for y in range(2):
                for z in range(4):
                    at = (x + shift[0], y + shift[1], z + shift[2])
                    side = tuple((-1 if c < 0 else 1 if c >= e else 0) for c, e in zip(at, (2, 2, 4)))
                    wrapped = tuple(c % e for c, e in zip(at, (2, 2, 4)))
                    row = SIDES.index(side) * 16 + piece_rows(side, COARSE).index(wrapped)
                    picks[number * 16 + x * 8 + y * 4 + z, row] = 1
    return picks


def fine_places():
    places = np.zeros((1, 1024), np.int32)
    for o, (a, b, c) in enumerate(OCTANTS):
        for x in range(4):
            for y in range(4):
                for z in range(8):
                    places[0, o * 128 + x * 32 + y * 8 + z] = ((2 * x + a) * 8 + 2 * y + b) * 16 + 2 * z + c
    return places


def coarse_picks():
    picks = np.zeros((128, 128), np.float32)
    for o, (a, b, c) in enumerate(OCTANTS):
        for x in range(2):
            for y in range(2):
                for z in range(4):
                    picks[o * 16 + x * 8 + y * 4 + z, ((2 * x + a) * 4 + 2 * y + b) * 8 + 2 * z + c] = 1
    return picks


def window_of(offset, octant):
    direction, source = [], []
    for d, a in zip(offset, octant):
        direction.append(min(1, max(-1, (a + d) // 2)))
        source.append((a + d) % 2)
    number = (direction[0] + 1) * 9 + (direction[1] + 1) * 3 + direction[2] + 1
    return number * 8 + source[0] * 4 + source[1] * 2 + source[2]


def kind(component):
    return 0 if abs(component) < 3 else component


def groups():
    by_kind = {}
    for offset in SHIFTS:
        by_kind.setdefault(tuple(kind(c) for c in offset), []).append(offset)

    def octants_of(kinds):
        return [o for o in OCTANTS if all(k == 0 or (k == 3) == (a == 0) for k, a in zip(kinds, o))]

    middle = by_kind[(0, 0, 0)]
    cuts = [[o for o in middle if o[0] == -2]]
    inner = [o for o in middle if abs(o[0]) < 2]
    cuts += [inner[:25], inner[25:] + [None, None], [o for o in middle if o[0] == 2]]
    eight = [(cut, OCTANTS) for cut in cuts]
    four, two = [], []
    for kinds, offsets in sorted(by_kind.items()):
        edges = sum(k != 0 for k in kinds)
        if edges == 1:
            four.append((offsets, octants_of(kinds)))
        if edges == 2:
            offsets = list(offsets)
            if kinds[2] == 0:
                offsets += by_kind[kinds[:2] + (-3,)] + by_kind[kinds[:2] + (3,)]
            two.append((offsets + [None] * (8 - len(offsets)), octants_of(kinds)))
    return eight, four, two


def table(members):
    slots, octants = [], []
    for offsets, octs in members:
        octants += [OCTANTS.index(o) for o in octs]
        for offset in offsets:
            if offset is None:
                slots += [NUMBER[offsets[0]], OFFS] + [window_of(offsets[0], o) for o in octs]
            else:
                slots += [NUMBER[offset], NUMBER[offset]] + [window_of(offset, o) for o in octs]
    return np.array(slots, np.int32), np.array(octants, np.int32)


EIGHT, FOUR, TWO = groups()


def coarse_table():
    return np.array(
        [
            window_of(offset or offsets[0], o)
            for members in (EIGHT, FOUR, TWO)
            for offsets, _ in members
            for offset in offsets
            for o in OCTANTS
        ],
        np.int32,
    )


TAILS = [
    offsets[at : at + 4]
    for members in (EIGHT, FOUR, TWO)
    for offsets, _ in members
    for at in range(0, len(offsets), 4)
]


PLANES = [(min(n for n, o in enumerate(SHIFTS) if o[0] == d), sum(o[0] == d for o in SHIFTS)) for d in range(-3, 4)]
PLANE_ORDER = [1, 2, 3, 4, 5, 0, 6]


def brick_of(me):
    def bit(place):
        return me // 2**place % 2

    return bit(2) + 2 * bit(5), bit(1) + 2 * bit(4), bit(0) + 2 * bit(3) + 4 * bit(6)


def neighbour(me, shift):
    x, y, z = [(c + d + e) % e for c, d, e in zip(brick_of(me), shift, (4, 4, 8))]
    return (
        z % 2 + 2 * (y % 2) + 4 * (x % 2) + 8 * (z // 2 % 2) + 16 * (y // 2) + 32 * (x // 2) + 64 * (z // 4)
    )


def inside(me, shift):
    found = True
    for c, d, e in zip(brick_of(me), shift, (4, 4, 8)):
        if d == 1:
            found = jnp.logical_and(found, c < e - 1)
        if d == -1:
            found = jnp.logical_and(found, c > 0)
    return found


def fold(piece, count):
    tiles, folds = folding(count)
    row = lax.broadcasted_iota(jnp.int32, (16, tiles * 128), 0) // count
    total = jnp.zeros((16, tiles * 128), F32)
    for number in range(folds):
        part = piece[:, number * tiles * 128 : min((number + 1) * tiles, 10) * 128]
        if part.shape[1] < tiles * 128:
            part = jnp.concatenate([part, jnp.zeros((16, tiles * 128 - part.shape[1]), F32)], axis=1)
        total = jnp.where(row == number, part, total)
    return total.astype(BF16)


def unfold(piece, count):
    folds = folding(count)[1]
    piece = piece.astype(F32)
    flat = jnp.concatenate([piece[k * count : (k + 1) * count] for k in range(folds)], axis=1)[:, :1280]
    return jnp.concatenate([flat, jnp.zeros((16 - count, 1280), F32)], axis=0).astype(BF16)


def spread_lanes(blocks, copies=False):
    gap = jnp.zeros((blocks[0].shape[0], 8), blocks[0].dtype)
    return jnp.concatenate([part for block in blocks for part in (block, gap)], axis=1)


def exchange_kernel(
    mult, up, picks, cpicks, cends, maps, ef, ec, heads, tails,
    sent, csent, slab, turned, turned_tail, whole_tail, head, tail, send, recv, csend, crecv, slab_sem, out_sem,
):
    me = lax.axis_index("curve")

    def fetch(i, size=16):
        return pltpu.make_async_copy(
            maps.at[pl.ds(i * 16, size)], slab.at[i % 2, pl.ds(0, size)], slab_sem.at[i % 2]
        )

    fetch(0).start()
    others = [s for s in SIDES if s != (0, 0, 0)]
    barrier = pltpu.get_barrier_semaphore()
    for side in others:
        pl.semaphore_signal(barrier, inc=1, device_id=(neighbour(me, side),), device_id_type=MESH)

    row = lax.broadcasted_iota(jnp.int32, (128, 1), 0)
    base = row // 32 * 256 + row // 8 % 4 * 32 + row % 8 * 2
    lane = lax.broadcasted_iota(jnp.int32, (128, 1024), 1)
    rests, coarse = [], jnp.zeros((128, Q), F32)
    for o, (a, b, c) in enumerate(OCTANTS):
        pick = (lane == base + (a * 128 + b * 16 + c)).astype(F32).astype(BF16)
        child = lax.dot_general(pick, mult[...], NT, preferred_element_type=F32)
        ef[OWN : OWN + 128, o * 128 : (o + 1) * 128] = child[:, :128].astype(BF16)
        rests.append(child[:, 128:])
        coarse += lax.dot_general(child.astype(BF16), up[o], NT, preferred_element_type=F32)
    ef[OWN : OWN + 128, 1024:1280] = spread_lanes(rests).astype(BF16)
    folded = [side for side in others if PLACES[side][1] == 16 and len(piece_rows(side)) < 16]
    pieces = lax.dot_general(picks[...], ef[OWN : OWN + 128, :], NN, preferred_element_type=F32)
    for side in others:
        start, size = PLACES[side]
        count = len(piece_rows(side))
        piece = pieces[start : start + size]
        tiles = folding(count)[0]
        sent[start : start + size, 0 : tiles * 128] = fold(piece, count) if side in folded else piece.astype(BF16)

        @pl.when(jnp.logical_not(inside(me, side)))
        def _(start=start, size=size, side=side):
            ef[start : start + size, :] = jnp.zeros((size, 1280), BF16)
            ec[SIDES.index(side)] = jnp.zeros((16, 1280), BF16)

    pl.semaphore_wait(barrier, 26)

    def fine_copy(number):
        side = others[number]
        start, size = PLACES[side]
        lanes = pl.ds(0, folding(len(piece_rows(side)))[0] * 128)
        return pltpu.make_async_remote_copy(
            src_ref=sent.at[pl.ds(start, size), lanes],
            dst_ref=ef.at[pl.ds(start, size), lanes],
            send_sem=send.at[number],
            recv_sem=recv.at[number],
            device_id=(neighbour(me, tuple(-c for c in side)),),
            device_id_type=MESH,
        )

    def coarse_copy(number):
        side = others[number]
        lanes = pl.ds(0, folding(len(piece_rows(side, COARSE)))[0] * 128)
        return pltpu.make_async_remote_copy(
            src_ref=csent.at[SIDES.index(side), :, lanes],
            dst_ref=ec.at[SIDES.index(side), :, lanes],
            send_sem=csend.at[number],
            recv_sem=crecv.at[number],
            device_id=(neighbour(me, tuple(-c for c in side)),),
            device_id_type=MESH,
        )

    def start_all(copy):
        for number, side in enumerate(others):

            @pl.when(inside(me, tuple(-c for c in side)))
            def _(number=number):
                copy(number).start()

    start_all(fine_copy)
    coarse = coarse.astype(BF16)
    rests = []
    mine = lax.dot_general(cpicks[...], coarse, NN, preferred_element_type=F32)
    for o in range(8):
        ec[13, :, o * 128 : (o + 1) * 128] = mine[o * 16 : (o + 1) * 16, :128].astype(BF16)
        rests.append(mine[o * 16 : (o + 1) * 16, 128:])
    ec[13, :, 1024:1280] = spread_lanes(rests).astype(BF16)
    pieces = lax.dot_general(cends[...], ec[13], NN, preferred_element_type=F32)
    for side in others:
        place, count = SIDES.index(side), len(piece_rows(side, COARSE))
        piece = pieces[place * 16 : place * 16 + 16]
        csent[place, :, 0 : folding(count)[0] * 128] = fold(piece, count)
    start_all(coarse_copy)

    def leave(i):
        rows = pl.ds(pl.multiple_of(i * 16, 16), 16)
        return [
            pltpu.make_async_copy(head.at[i % 2], heads.at[:, rows], out_sem.at[0, i % 2]),
            pltpu.make_async_copy(tail.at[i % 2], tails.at[:, rows], out_sem.at[1, i % 2]),
        ]

    gap = jnp.zeros((8, OFFS), F32)
    quarter = lax.broadcasted_iota(jnp.int32, (16, 128), 1) // 32

    def step(i, _):
        @pl.when(i < 9)
        def _():
            fetch(i).wait()

        @pl.when(i == 9)
        def _():
            fetch(9, 8).wait()

        @pl.when(i < 8)
        def _():
            fetch(i + 1).start()

        @pl.when(i == 8)
        def _():
            fetch(9, 8).start()

        @pl.when(i >= 2)
        def _():
            for part in leave(i - 2):
                part.wait()

        def one(p, _):
            turned[p, 0:OFFS, :] = jnp.swapaxes(slab[i % 2, p, 0:128], 0, 1).astype(F32)
            last = slab[i % 2, p, 128:Q].astype(F32)
            last = jnp.concatenate([last, gap] * 4, axis=0).astype(BF16)
            turned_tail[p, 0:OFFS, :] = jnp.swapaxes(last, 0, 1).astype(F32)
            return 0

        lax.fori_loop(0, 16, one, 0, unroll=8)

        def eight(k, _):
            at = pl.ds(pl.multiple_of(k * 8, 8), 8)
            head[i % 2, at] = jnp.swapaxes(turned[:, at, :], 0, 1).astype(BF16)
            whole_tail[at] = jnp.swapaxes(turned_tail[:, at, :], 0, 1)
            return 0

        lax.fori_loop(0, 40, eight, 0, unroll=10)
        for number, slots in enumerate(TAILS):
            total = jnp.zeros((16, 128), F32)
            for j, offset in enumerate(slots):
                if offset is not None:
                    total = jnp.where(quarter == j, whole_tail[NUMBER[offset]], total)
            tail[i % 2, number] = total.astype(BF16)
        for part in leave(i):
            part.start()
        return 0

    lax.fori_loop(0, 10, step, 0)
    for part in leave(8) + leave(9):
        part.wait()
    for copy in (fine_copy, coarse_copy):
        for number, side in enumerate(others):

            @pl.when(inside(me, tuple(-c for c in side)))
            def _(copy=copy, number=number):
                copy(number).wait_send()

            @pl.when(inside(me, side))
            def _(copy=copy, number=number):
                copy(number).wait_recv()

    for side in folded:
        rows, count = slice(PLACES[side][0], PLACES[side][0] + 16), len(piece_rows(side))
        ef[rows, :] = unfold(ef[rows, 0 : folding(count)[0] * 128], count)
    for side in others:
        place, count = SIDES.index(side), len(piece_rows(side, COARSE))
        ec[place] = unfold(ec[place, :, 0 : folding(count)[0] * 128], count)


def exchange(multipole, upward_maps, maps):
    vmem = pl.BlockSpec(memory_space=pltpu.VMEM)
    return pl.pallas_call(
        exchange_kernel,
        out_shape=[
            jax.ShapeDtypeStruct((ROWS, 1280), BF16),
            jax.ShapeDtypeStruct((27, 16, 1280), BF16),
            jax.ShapeDtypeStruct((OFFS + 4, 160, 128), BF16),
            jax.ShapeDtypeStruct((len(TAILS), 160, 128), BF16),
        ],
        in_specs=[vmem] * 5 + [pl.BlockSpec(memory_space=pl.ANY)],
        out_specs=[vmem] * 2 + [pl.BlockSpec(memory_space=pl.ANY)] * 2,
        scratch_shapes=[
            pltpu.VMEM((ROWS, 1280), BF16),
            pltpu.VMEM((27, 16, 640), BF16),
            pltpu.VMEM((2, 16, Q, OFFS), BF16),
            pltpu.VMEM((16, OFFS + 4, 128), F32),
            pltpu.VMEM((16, OFFS + 4, 128), F32),
            pltpu.VMEM((OFFS + 4, 16, 128), F32),
            pltpu.VMEM((2, OFFS + 4, 16, 128), BF16),
            pltpu.VMEM((2, len(TAILS), 16, 128), BF16),
            pltpu.SemaphoreType.DMA((26,)),
            pltpu.SemaphoreType.DMA((26,)),
            pltpu.SemaphoreType.DMA((26,)),
            pltpu.SemaphoreType.DMA((26,)),
            pltpu.SemaphoreType.DMA((2,)),
            pltpu.SemaphoreType.DMA((2, 2)),
        ],
        compiler_params=pltpu.CompilerParams(
            collective_id=0, has_side_effects=True, vmem_limit_bytes=40 << 20
        ),
        name="exchange",
    )(
        multipole, upward_maps, jnp.asarray(send_picks(), BF16), jnp.asarray(coarse_picks(), BF16),
        jnp.asarray(coarse_send_picks(), BF16), jnp.transpose(maps, (1, 2, 0)),
    )


def translate_kernel(
    t8, o8, t4, o4, t2, o2, tc, ef, ec, heads_in, tails_in, fine_lists, coarse_lists, down, inverse,
    wrows, wcpicks, places, cpicks, out,
    heads, tails, pick, window, cmain, crest, mask, cmask, perm, lhs, acc, cacc, sems,
):
    loads = [
        pltpu.make_async_copy(heads_in.at[pl.ds(*PLANES[n])], heads.at[pl.ds(*PLANES[n])], sems.at[n])
        for n in range(7)
    ]
    load_tails = pltpu.make_async_copy(tails_in, tails, sems.at[7])
    load_tails.start()
    for n in PLANE_ORDER:
        loads[n].start()

    for at in range(0, 1024, 128):
        box = lax.broadcasted_iota(jnp.int32, (128, 1024), 0) + at
        perm[at : at + 128, :] = (box == places[...]).astype(F32).astype(BF16)

    present = (fine_lists[...] >= 0).astype(F32).astype(BF16)
    for o in range(8):
        mask[o, 0:OFFS, :] = lax.dot_general(
            present, perm[:, o * 128 : (o + 1) * 128], NN, preferred_element_type=F32
        )
        mask[o, OFFS : OFFS + 4, :] = jnp.zeros((4, 128), F32)
    picks = cpicks[...].reshape(128, 128)
    present = (coarse_lists[...] >= 0).astype(F32).astype(BF16)
    cmask[0:OFFS, :] = lax.dot_general(present, picks, NT, preferred_element_type=F32)
    cmask[OFFS : OFFS + 4, :] = jnp.zeros((4, 128), F32)

    for dx in (-1, 0, 1):
        first, last = SPAN[dx]
        span = last - first

        def mark(i, _, first=first, dx=dx):
            iota = lax.broadcasted_iota(jnp.int32, (16, 1152), 0) + (first + i * 16)
            wanted = wrows[:, (dx + 1) * 1152 : (dx + 2) * 1152]
            at = pl.ds(pl.multiple_of(i * 16, 16), 16)
            pick[at, :] = (iota == wanted).astype(F32).astype(BF16)
            return 0

        lax.fori_loop(0, span // 16, mark, 0)

        def block(i, _, first=first, last=last, span=span, dx=dx):
            lanes = pl.ds(pl.multiple_of(i * 128, 128), 128)
            got = lax.dot_general(
                ef[first:last, lanes], pick[0:span, :], TN, preferred_element_type=F32
            ).astype(BF16)
            for n in range(9):
                window[((dx + 1) * 9 + n) * 8 + i, 0:128, :] = got[:, n * 128 : (n + 1) * 128]
            return 0

        lax.fori_loop(0, 8, block, 0)
        for half in range(2):
            got = lax.dot_general(
                ef[first:last, 1024 + half * 128 : 1152 + half * 128], pick[0:span, :], TN, preferred_element_type=F32
            ).astype(BF16)
            for n in range(9):
                for c in range(4):
                    window[((dx + 1) * 9 + n) * 8 + half * 4 + c, 128:160, :] = got[
                        c * 32 : (c + 1) * 32, n * 128 : (n + 1) * 128
                    ]

    source = ec[...].reshape(27 * 16, 1280)
    for c in range(8):
        got = lax.dot_general(
            wcpicks[...], source[:, c * 128 : (c + 1) * 128], NN, preferred_element_type=F32
        ).astype(BF16)
        rest = lax.dot_general(
            wcpicks[...], source[:, 1024 + c * 32 : 1056 + c * 32], NN, preferred_element_type=F32
        )
        rest = jnp.concatenate([rest] * 4, axis=1).astype(BF16)
        group_of_lane = lax.broadcasted_iota(jnp.int32, (16, 128), 1) // 32
        for n in range(27):
            cmain[n * 8 + c] = got[n * 16 : (n + 1) * 16]
            for j in range(4):
                only = (group_of_lane == j).astype(F32).astype(BF16)
                crest[j, n * 8 + c] = rest[n * 16 : (n + 1) * 16] * only

    acc[...] = jnp.zeros_like(acc)
    cacc[...] = jnp.zeros_like(cacc)
    def body(i, tab, octs, slots, n, first_tail, first_slot):
        rests = -(-slots // 4)
        cut = slots // 2 + 1 if slots > 8 else slots
        kept = 16 - cut if slots > 8 else rests
        order = [("head", j) for j in range(cut)] + [("tail", g) for g in range(kept)]
        order += [("head", j) for j in range(cut, slots)] + [("tail", g) for g in range(kept, rests)]
        place = {block: number for number, block in enumerate(order)}
        width = len(order) * 128
        at = [(i * slots + j) * (2 + n) for j in range(slots)]
        km = [tab[a] for a in at]
        kk = [tab[a + 1] for a in at]
        members = [range(4 * g, min(4 * g + 4, slots)) for g in range(rests)]

        def span(kind, number):
            return slice(place[kind, number] * 128, place[kind, number] * 128 + 128)

        for j in range(slots):
            lhs[:, span("head", j)] = heads[km[j], 0:Q, :]
        for g in range(rests):
            lhs[:, span("tail", g)] = tails[first_tail + i * rests + g, 0:Q, :]

        def shown(q, blocks):
            o = octs[i * n + q]
            parts = []
            for kind, number in blocks:
                for j in [number] if kind == "head" else members[number]:
                    w = tab[at[j] + 2 + q]
                    m = jnp.broadcast_to(mask[o, pl.ds(kk[j], 1), :], (16, 128)).astype(BF16)
                    if kind == "head":
                        parts.append(window[w, 0:128, :] * jnp.concatenate([m] * 8, axis=0))
                    else:
                        parts.append(window[w, 128:160, :] * jnp.concatenate([m] * 2, axis=0))
                if kind == "tail" and len(members[number]) < 4:
                    parts.append(jnp.zeros((128 - 32 * len(members[number]), 128), BF16))
            return jnp.concatenate(parts, axis=0)

        for q in range(0, n, PAIR):
            got = None
            for first in range(0, width, DEEP):
                last = min(first + DEEP, width)
                blocks = order[first // 128 : last // 128]
                masked = jnp.concatenate([shown(q + h, blocks) for h in range(PAIR)], axis=1)
                term = lax.dot_general(lhs[:, first:last], masked, NN, preferred_element_type=F32)
                got = term if got is None else got + term
            for h in range(PAIR):
                acc[octs[i * n + q + h]] += got[:, h * 128 : h * 128 + 128]

        total = jnp.zeros((Q, 128), F32)
        for j in range(slots):
            first = (first_slot + i * slots + j) * 8
            ws = [tc[first + q] for q in range(8)]
            seen = jnp.concatenate(
                [
                    jnp.concatenate([cmain[w] for w in ws], axis=0),
                    jnp.concatenate([crest[j % 4, w] for w in ws], axis=0),
                ],
                axis=1,
            )
            both = jnp.concatenate([lhs[:, span("head", j)], lhs[:, span("tail", j // 4)]], axis=1)
            term = lax.dot_general(both, seen, NT, preferred_element_type=F32)
            total += term * cmask[pl.ds(kk[j], 1), :]
        cacc[...] += total

    def eight(i, _):
        for step, planes in enumerate(((1,), (2, 3), (4,), (5, 0, 6))):

            @pl.when(i == step)
            def _(planes=planes):
                for n in planes:
                    loads[n].wait()

        body(i, t8, o8, 25, 8, 0, 0)
        return 0

    load_tails.wait()
    lax.fori_loop(0, 4, eight, 0)

    def four(i, _):
        body(i, t4, o4, 25, 4, 28, 100)
        return 0

    lax.fori_loop(0, 6, four, 0)

    def two(i, _):
        body(i, t2, o2, 8, 2, 70, 250)
        return 0

    lax.fori_loop(0, 12, two, 0)

    local = lax.dot_general(
        (0.5 * cacc[...]).astype(BF16), picks, NN, preferred_element_type=F32
    ).astype(BF16)
    for o in range(8):
        total = acc[o] + lax.dot_general(down[o], local, NN, preferred_element_type=F32)
        density = lax.dot_general(inverse[...], total.astype(BF16), NN, preferred_element_type=F32)
        lhs[:, o * 128 : (o + 1) * 128] = density.astype(BF16)
    out[...] = lax.dot_general(lhs[:, 0:1024], perm[...], NT, preferred_element_type=F32).astype(BF16)


def translate(ef, ec, heads, tails, fine_lists, coarse_lists, down, inverse):
    vmem = pl.BlockSpec(memory_space=pltpu.VMEM)
    smem = pl.BlockSpec(memory_space=pltpu.SMEM)
    tables = [jnp.asarray(part) for members in (EIGHT, FOUR, TWO) for part in table(members)]
    return pl.pallas_call(
        translate_kernel,
        out_shape=jax.ShapeDtypeStruct((Q, 1024), BF16),
        in_specs=[smem] * 7 + [vmem] * 2 + [pl.BlockSpec(memory_space=pl.ANY)] * 2 + [vmem] * 8,
        out_specs=vmem,
        scratch_shapes=[
            pltpu.VMEM((OFFS + 4, 160, 128), BF16),
            pltpu.VMEM((len(TAILS), 160, 128), BF16),
            pltpu.VMEM((448, 1152), BF16),
            pltpu.VMEM((216, 160, 128), BF16),
            pltpu.VMEM((216, 16, 128), BF16),
            pltpu.VMEM((4, 216, 16, 128), BF16),
            pltpu.VMEM((8, OFFS + 4, 128), F32),
            pltpu.VMEM((OFFS + 4, 128), F32),
            pltpu.VMEM((1024, 1024), BF16),
            pltpu.VMEM((Q, 4096), BF16),
            pltpu.VMEM((8, Q, 128), F32),
            pltpu.VMEM((Q, 128), F32),
            pltpu.SemaphoreType.DMA((8,)),
        ],
        compiler_params=pltpu.CompilerParams(vmem_limit_bytes=62 << 20),
        name="translate",
    )(
        *tables, jnp.asarray(coarse_table()), ef, ec, heads, tails, fine_lists, coarse_lists, down, inverse,
        jnp.asarray(window_rows().reshape(1, -1)), jnp.asarray(coarse_window_picks(), BF16),
        jnp.asarray(fine_places()), jnp.asarray(coarse_picks().reshape(8, 16, 128), BF16),
    )


def local(multipole, upward_maps, transfer_maps, downward_maps, check_inverse, fine_lists, coarse_lists):
    ef, ec, heads, tails = exchange(multipole, upward_maps, transfer_maps)
    return translate(ef, ec, heads, tails, fine_lists, coarse_lists, downward_maps, check_inverse)


def solution(mesh):
    placed = (P(None, "curve"), P(), P(), P(), P(), P(None, "curve"), P(None, "curve"))
    return jax.shard_map(local, mesh=mesh, in_specs=placed, out_specs=P(None, "curve"), check_vma=False)
```

```python
import functools

import jax
import jax.numpy as jnp
import numpy as np
from jax import lax
from jax.experimental import pallas as pl
from jax.experimental.pallas import tpu as pltpu
from jax.sharding import PartitionSpec as P

Q = 152
OFFS = 316
F32 = jnp.float32
BF16 = jnp.bfloat16
PAIR, DEEP = 2, 512
NN = (((1,), (0,)), ((), ()))
NT = (((1,), (1,)), ((), ()))
TN = (((0,), (0,)), ((), ()))
MESH = pl.DeviceIdType.MESH

SHIFTS = [
    (i, j, k)
    for i in range(-3, 4)
    for j in range(-3, 4)
    for k in range(-3, 4)
    if max(abs(i), abs(j), abs(k)) >= 2
]
NUMBER = {offset: number for number, offset in enumerate(SHIFTS)}
SIDES = [(i, j, k) for i in (-1, 0, 1) for j in (-1, 0, 1) for k in (-1, 0, 1)]
OCTANTS = [(a, b, c) for a in (0, 1) for b in (0, 1) for c in (0, 1)]


FINE = (4, 4, 8)
COARSE = (2, 2, 4)


def piece_rows(side, extents=FINE):
    ranges = []
    for component, extent in zip(side, extents):
        ranges.append({-1: [extent - 1], 0: list(range(extent)), 1: [0]}[component])
    return [(x, y, z) for x in ranges[0] for y in ranges[1] for z in ranges[2]]


def folding(count):
    tiles = {8: 5, 4: 3, 2: 2, 1: 1}.get(count, 10)
    return tiles, -(-10 // tiles)


def piece_places():
    places, row = {}, 0
    order = [s for s in SIDES if s[0] == -1] + [(0, 0, 0)] + [s for s in SIDES if s[0] == 0 and s != (0, 0, 0)]
    order += [s for s in SIDES if s[0] == 1]
    for side in order:
        size = -(-len(piece_rows(side)) // 16) * 16
        places[side] = (row, size)
        row += size
    return places, row


PLACES, ROWS = piece_places()
OWN = PLACES[(0, 0, 0)][0]
SPAN = {-1: (0, OWN + 288), 0: (OWN, OWN + 288), 1: (OWN, ROWS)}


def piece_picks(side, extents, size):
    picks = np.zeros((size, extents[0] * extents[1] * extents[2]), np.float32)
    rows = piece_rows(side, extents)
    for fold in range(folding(len(rows))[1]):
        for number, (x, y, z) in enumerate(rows):
            picks[fold * len(rows) + number, (x * extents[1] + y) * extents[2] + z] = 1
    return picks


def send_picks():
    picks = np.zeros((ROWS, 128), np.float32)
    for side, (row, size) in PLACES.items():
        picks[row : row + size] = piece_picks(side, FINE, size)
    return picks


def coarse_send_picks():
    return np.concatenate([piece_picks(side, COARSE, 16) for side in SIDES])


def window_rows():
    rows = np.zeros((27, 128), np.int32)
    for number, shift in enumerate(SIDES):
        for x in range(4):
            for y in range(4):
                for z in range(8):
                    at = (x + shift[0], y + shift[1], z + shift[2])
                    side = tuple((-1 if c < 0 else 1 if c >= e else 0) for c, e in zip(at, (4, 4, 8)))
                    wrapped = tuple(c % e for c, e in zip(at, (4, 4, 8)))
                    rows[number, x * 32 + y * 8 + z] = PLACES[side][0] + piece_rows(side).index(wrapped)
    return rows


def coarse_window_picks():
    picks = np.zeros((27 * 16, 27 * 16), np.float32)
    for number, shift in enumerate(SIDES):
        for x in range(2):
            for y in range(2):
                for z in range(4):
                    at = (x + shift[0], y + shift[1], z + shift[2])
                    side = tuple((-1 if c < 0 else 1 if c >= e else 0) for c, e in zip(at, (2, 2, 4)))
                    wrapped = tuple(c % e for c, e in zip(at, (2, 2, 4)))
                    row = SIDES.index(side) * 16 + piece_rows(side, COARSE).index(wrapped)
                    picks[number * 16 + x * 8 + y * 4 + z, row] = 1
    return picks


def fine_places():
    places = np.zeros((1, 1024), np.int32)
    for o, (a, b, c) in enumerate(OCTANTS):
        for x in range(4):
            for y in range(4):
                for z in range(8):
                    places[0, o * 128 + x * 32 + y * 8 + z] = ((2 * x + a) * 8 + 2 * y + b) * 16 + 2 * z + c
    return places


def coarse_picks():
    picks = np.zeros((128, 128), np.float32)
    for o, (a, b, c) in enumerate(OCTANTS):
        for x in range(2):
            for y in range(2):
                for z in range(4):
                    picks[o * 16 + x * 8 + y * 4 + z, ((2 * x + a) * 4 + 2 * y + b) * 8 + 2 * z + c] = 1
    return picks


def window_of(offset, octant):
    direction, source = [], []
    for d, a in zip(offset, octant):
        direction.append(min(1, max(-1, (a + d) // 2)))
        source.append((a + d) % 2)
    number = (direction[0] + 1) * 9 + (direction[1] + 1) * 3 + direction[2] + 1
    return number * 8 + source[0] * 4 + source[1] * 2 + source[2]


def kind(component):
    return 0 if abs(component) < 3 else component


def groups():
    by_kind = {}
    for offset in SHIFTS:
        by_kind.setdefault(tuple(kind(c) for c in offset), []).append(offset)

    def octants_of(kinds):
        return [o for o in OCTANTS if all(k == 0 or (k == 3) == (a == 0) for k, a in zip(kinds, o))]

    middle = by_kind[(0, 0, 0)]
    cuts = [[o for o in middle if o[0] == -2]]
    inner = [o for o in middle if abs(o[0]) < 2]
    cuts += [inner[:25], inner[25:] + [None, None], [o for o in middle if o[0] == 2]]
    eight = [(cut, OCTANTS) for cut in cuts]
    four, two = [], []
    for kinds, offsets in sorted(by_kind.items()):
        edges = sum(k != 0 for k in kinds)
        if edges == 1:
            four.append((offsets, octants_of(kinds)))
        if edges == 2:
            offsets = list(offsets)
            if kinds[2] == 0:
                offsets += by_kind[kinds[:2] + (-3,)] + by_kind[kinds[:2] + (3,)]
            two.append((offsets + [None] * (8 - len(offsets)), octants_of(kinds)))
    return eight, four, two


def table(members):
    slots, octants = [], []
    for offsets, octs in members:
        octants += [OCTANTS.index(o) for o in octs]
        for offset in offsets:
            if offset is None:
                slots += [NUMBER[offsets[0]], OFFS] + [window_of(offsets[0], o) for o in octs]
            else:
                slots += [NUMBER[offset], NUMBER[offset]] + [window_of(offset, o) for o in octs]
    return np.array(slots, np.int32), np.array(octants, np.int32)


EIGHT, FOUR, TWO = groups()


def coarse_table():
    return np.array(
        [
            window_of(offset or offsets[0], o)
            for members in (EIGHT, FOUR, TWO)
            for offsets, _ in members
            for offset in offsets
            for o in OCTANTS
        ],
        np.int32,
    )


TAILS = [
    offsets[at : at + 4]
    for members in (EIGHT, FOUR, TWO)
    for offsets, _ in members
    for at in range(0, len(offsets), 4)
]


PLANES = [(min(n for n, o in enumerate(SHIFTS) if o[0] == d), sum(o[0] == d for o in SHIFTS)) for d in range(-3, 4)]
PLANE_ORDER = [1, 2, 3, 4, 5, 0, 6]


def brick_of(me):
    def bit(place):
        return me // 2**place % 2

    return bit(2) + 2 * bit(5), bit(1) + 2 * bit(4), bit(0) + 2 * bit(3) + 4 * bit(6)


def neighbour(me, shift):
    x, y, z = [(c + d + e) % e for c, d, e in zip(brick_of(me), shift, (4, 4, 8))]
    return (
        z % 2 + 2 * (y % 2) + 4 * (x % 2) + 8 * (z // 2 % 2) + 16 * (y // 2) + 32 * (x // 2) + 64 * (z // 4)
    )


def inside(me, shift):
    found = True
    for c, d, e in zip(brick_of(me), shift, (4, 4, 8)):
        if d == 1:
            found = jnp.logical_and(found, c < e - 1)
        if d == -1:
            found = jnp.logical_and(found, c > 0)
    return found


def fold(piece, count):
    tiles, folds = folding(count)
    row = lax.broadcasted_iota(jnp.int32, (16, tiles * 128), 0) // count
    total = jnp.zeros((16, tiles * 128), F32)
    for number in range(folds):
        part = piece[:, number * tiles * 128 : min((number + 1) * tiles, 10) * 128]
        if part.shape[1] < tiles * 128:
            part = jnp.concatenate([part, jnp.zeros((16, tiles * 128 - part.shape[1]), F32)], axis=1)
        total = jnp.where(row == number, part, total)
    return total.astype(BF16)


def unfold(piece, count):
    folds = folding(count)[1]
    piece = piece.astype(F32)
    flat = jnp.concatenate([piece[k * count : (k + 1) * count] for k in range(folds)], axis=1)[:, :1280]
    return jnp.concatenate([flat, jnp.zeros((16 - count, 1280), F32)], axis=0).astype(BF16)


def spread_lanes(blocks, copies=False):
    gap = jnp.zeros((blocks[0].shape[0], 8), blocks[0].dtype)
    return jnp.concatenate([part for block in blocks for part in (block, gap)], axis=1)


def exchange_kernel(
    mult, up, picks, cpicks, cends, maps, ef, ec, heads, tails,
    sent, csent, slab, turned, turned_tail, whole_tail, head, tail, send, recv, csend, crecv, slab_sem, out_sem,
):
    me = lax.axis_index("curve")

    def fetch(i, size=16):
        return pltpu.make_async_copy(
            maps.at[pl.ds(i * 16, size)], slab.at[i % 2, pl.ds(0, size)], slab_sem.at[i % 2]
        )

    fetch(0).start()
    others = [s for s in SIDES if s != (0, 0, 0)]
    barrier = pltpu.get_barrier_semaphore()
    for side in others:
        pl.semaphore_signal(barrier, inc=1, device_id=(neighbour(me, side),), device_id_type=MESH)

    row = lax.broadcasted_iota(jnp.int32, (128, 1), 0)
    base = row // 32 * 256 + row // 8 % 4 * 32 + row % 8 * 2
    lane = lax.broadcasted_iota(jnp.int32, (128, 1024), 1)
    rests, coarse = [], jnp.zeros((128, Q), F32)
    for o, (a, b, c) in enumerate(OCTANTS):
        pick = (lane == base + (a * 128 + b * 16 + c)).astype(F32).astype(BF16)
        child = lax.dot_general(pick, mult[...], NT, preferred_element_type=F32)
        ef[OWN : OWN + 128, o * 128 : (o + 1) * 128] = child[:, :128].astype(BF16)
        rests.append(child[:, 128:])
        coarse += lax.dot_general(child.astype(BF16), up[o], NT, preferred_element_type=F32)
    ef[OWN : OWN + 128, 1024:1280] = spread_lanes(rests).astype(BF16)
    folded = [side for side in others if PLACES[side][1] == 16 and len(piece_rows(side)) < 16]
    pieces = lax.dot_general(picks[...], ef[OWN : OWN + 128, :], NN, preferred_element_type=F32)
    for side in others:
        start, size = PLACES[side]
        count = len(piece_rows(side))
        piece = pieces[start : start + size]
        tiles = folding(count)[0]
        sent[start : start + size, 0 : tiles * 128] = fold(piece, count) if side in folded else piece.astype(BF16)

        @pl.when(jnp.logical_not(inside(me, side)))
        def _(start=start, size=size, side=side):
            ef[start : start + size, :] = jnp.zeros((size, 1280), BF16)
            ec[SIDES.index(side)] = jnp.zeros((16, 1280), BF16)

    pl.semaphore_wait(barrier, 26)

    def fine_copy(number):
        side = others[number]
        start, size = PLACES[side]
        lanes = pl.ds(0, folding(len(piece_rows(side)))[0] * 128)
        return pltpu.make_async_remote_copy(
            src_ref=sent.at[pl.ds(start, size), lanes],
            dst_ref=ef.at[pl.ds(start, size), lanes],
            send_sem=send.at[number],
            recv_sem=recv.at[number],
            device_id=(neighbour(me, tuple(-c for c in side)),),
            device_id_type=MESH,
        )

    def coarse_copy(number):
        side = others[number]
        lanes = pl.ds(0, folding(len(piece_rows(side, COARSE)))[0] * 128)
        return pltpu.make_async_remote_copy(
            src_ref=csent.at[SIDES.index(side), :, lanes],
            dst_ref=ec.at[SIDES.index(side), :, lanes],
            send_sem=csend.at[number],
            recv_sem=crecv.at[number],
            device_id=(neighbour(me, tuple(-c for c in side)),),
            device_id_type=MESH,
        )

    def start_all(copy):
        for number, side in enumerate(others):

            @pl.when(inside(me, tuple(-c for c in side)))
            def _(number=number):
                copy(number).start()

    start_all(fine_copy)
    coarse = coarse.astype(BF16)
    rests = []
    mine = lax.dot_general(cpicks[...], coarse, NN, preferred_element_type=F32)
    for o in range(8):
        ec[13, :, o * 128 : (o + 1) * 128] = mine[o * 16 : (o + 1) * 16, :128].astype(BF16)
        rests.append(mine[o * 16 : (o + 1) * 16, 128:])
    ec[13, :, 1024:1280] = spread_lanes(rests).astype(BF16)
    pieces = lax.dot_general(cends[...], ec[13], NN, preferred_element_type=F32)
    for side in others:
        place, count = SIDES.index(side), len(piece_rows(side, COARSE))
        piece = pieces[place * 16 : place * 16 + 16]
        csent[place, :, 0 : folding(count)[0] * 128] = fold(piece, count)
    start_all(coarse_copy)

    def leave(i):
        rows = pl.ds(pl.multiple_of(i * 16, 16), 16)
        return [
            pltpu.make_async_copy(head.at[i % 2], heads.at[:, rows], out_sem.at[0, i % 2]),
            pltpu.make_async_copy(tail.at[i % 2], tails.at[:, rows], out_sem.at[1, i % 2]),
        ]

    gap = jnp.zeros((8, OFFS), F32)
    quarter = lax.broadcasted_iota(jnp.int32, (16, 128), 1) // 32

    def step(i, _):
        @pl.when(i < 9)
        def _():
            fetch(i).wait()

        @pl.when(i == 9)
        def _():
            fetch(9, 8).wait()

        @pl.when(i < 8)
        def _():
            fetch(i + 1).start()

        @pl.when(i == 8)
        def _():
            fetch(9, 8).start()

        @pl.when(i >= 2)
        def _():
            for part in leave(i - 2):
                part.wait()

        def one(p, _):
            turned[p, 0:OFFS, :] = jnp.swapaxes(slab[i % 2, p, 0:128], 0, 1).astype(F32)
            last = slab[i % 2, p, 128:Q].astype(F32)
            last = jnp.concatenate([last, gap] * 4, axis=0).astype(BF16)
            turned_tail[p, 0:OFFS, :] = jnp.swapaxes(last, 0, 1).astype(F32)
            return 0

        lax.fori_loop(0, 16, one, 0, unroll=16)

        def eight(k, _):
            at = pl.ds(pl.multiple_of(k * 8, 8), 8)
            head[i % 2, at] = jnp.swapaxes(turned[:, at, :], 0, 1).astype(BF16)
            whole_tail[at] = jnp.swapaxes(turned_tail[:, at, :], 0, 1)
            return 0

        lax.fori_loop(0, 40, eight, 0, unroll=20)
        for number, slots in enumerate(TAILS):
            total = jnp.zeros((16, 128), F32)
            for j, offset in enumerate(slots):
                if offset is not None:
                    total = jnp.where(quarter == j, whole_tail[NUMBER[offset]], total)
            tail[i % 2, number] = total.astype(BF16)
        for part in leave(i):
            part.start()
        return 0

    lax.fori_loop(0, 10, step, 0)
    for part in leave(8) + leave(9):
        part.wait()
    for copy in (fine_copy, coarse_copy):
        for number, side in enumerate(others):

            @pl.when(inside(me, tuple(-c for c in side)))
            def _(copy=copy, number=number):
                copy(number).wait_send()

            @pl.when(inside(me, side))
            def _(copy=copy, number=number):
                copy(number).wait_recv()

    for side in folded:
        rows, count = slice(PLACES[side][0], PLACES[side][0] + 16), len(piece_rows(side))
        ef[rows, :] = unfold(ef[rows, 0 : folding(count)[0] * 128], count)
    for side in others:
        place, count = SIDES.index(side), len(piece_rows(side, COARSE))
        ec[place] = unfold(ec[place, :, 0 : folding(count)[0] * 128], count)


def exchange(multipole, upward_maps, maps):
    vmem = pl.BlockSpec(memory_space=pltpu.VMEM)
    return pl.pallas_call(
        exchange_kernel,
        out_shape=[
            jax.ShapeDtypeStruct((ROWS, 1280), BF16),
            jax.ShapeDtypeStruct((27, 16, 1280), BF16),
            jax.ShapeDtypeStruct((OFFS + 4, 160, 128), BF16),
            jax.ShapeDtypeStruct((len(TAILS), 160, 128), BF16),
        ],
        in_specs=[vmem] * 5 + [pl.BlockSpec(memory_space=pl.ANY)],
        out_specs=[vmem] * 2 + [pl.BlockSpec(memory_space=pl.ANY)] * 2,
        scratch_shapes=[
            pltpu.VMEM((ROWS, 1280), BF16),
            pltpu.VMEM((27, 16, 640), BF16),
            pltpu.VMEM((2, 16, Q, OFFS), BF16),
            pltpu.VMEM((16, OFFS + 4, 128), F32),
            pltpu.VMEM((16, OFFS + 4, 128), F32),
            pltpu.VMEM((OFFS + 4, 16, 128), F32),
            pltpu.VMEM((2, OFFS + 4, 16, 128), BF16),
            pltpu.VMEM((2, len(TAILS), 16, 128), BF16),
            pltpu.SemaphoreType.DMA((26,)),
            pltpu.SemaphoreType.DMA((26,)),
            pltpu.SemaphoreType.DMA((26,)),
            pltpu.SemaphoreType.DMA((26,)),
            pltpu.SemaphoreType.DMA((2,)),
            pltpu.SemaphoreType.DMA((2, 2)),
        ],
        compiler_params=pltpu.CompilerParams(
            collective_id=0, has_side_effects=True, vmem_limit_bytes=40 << 20
        ),
        name="exchange",
    )(
        multipole, upward_maps, jnp.asarray(send_picks(), BF16), jnp.asarray(coarse_picks(), BF16),
        jnp.asarray(coarse_send_picks(), BF16), jnp.transpose(maps, (1, 2, 0)),
    )


def translate_kernel(
    t8, o8, t4, o4, t2, o2, tc, ef, ec, heads_in, tails_in, fine_lists, coarse_lists, down, inverse,
    wrows, wcpicks, places, cpicks, out,
    heads, tails, pick, window, cmain, crest, mask, cmask, perm, lhs, acc, cacc, sems,
):
    loads = [
        pltpu.make_async_copy(heads_in.at[pl.ds(*PLANES[n])], heads.at[pl.ds(*PLANES[n])], sems.at[n])
        for n in range(7)
    ]
    load_tails = pltpu.make_async_copy(tails_in, tails, sems.at[7])
    load_tails.start()
    for n in PLANE_ORDER:
        loads[n].start()

    for at in range(0, 1024, 128):
        box = lax.broadcasted_iota(jnp.int32, (128, 1024), 0) + at
        perm[at : at + 128, :] = (box == places[...]).astype(F32).astype(BF16)

    present = (fine_lists[...] >= 0).astype(F32).astype(BF16)
    for o in range(8):
        mask[o, 0:OFFS, :] = lax.dot_general(
            present, perm[:, o * 128 : (o + 1) * 128], NN, preferred_element_type=F32
        )
        mask[o, OFFS : OFFS + 4, :] = jnp.zeros((4, 128), F32)
    picks = cpicks[...].reshape(128, 128)
    present = (coarse_lists[...] >= 0).astype(F32).astype(BF16)
    cmask[0:OFFS, :] = lax.dot_general(present, picks, NT, preferred_element_type=F32)
    cmask[OFFS : OFFS + 4, :] = jnp.zeros((4, 128), F32)

    for dx in (-1, 0, 1):
        first, last = SPAN[dx]
        span = last - first

        def mark(i, _, first=first, dx=dx):
            iota = lax.broadcasted_iota(jnp.int32, (16, 1152), 0) + (first + i * 16)
            wanted = wrows[:, (dx + 1) * 1152 : (dx + 2) * 1152]
            at = pl.ds(pl.multiple_of(i * 16, 16), 16)
            pick[at, :] = (iota == wanted).astype(F32).astype(BF16)
            return 0

        lax.fori_loop(0, span // 16, mark, 0, unroll=2)

        def block(i, _, first=first, last=last, span=span, dx=dx):
            lanes = pl.ds(pl.multiple_of(i * 128, 128), 128)
            got = lax.dot_general(
                ef[first:last, lanes], pick[0:span, :], TN, preferred_element_type=F32
            ).astype(BF16)
            for n in range(9):
                window[((dx + 1) * 9 + n) * 8 + i, 0:128, :] = got[:, n * 128 : (n + 1) * 128]
            return 0

        lax.fori_loop(0, 8, block, 0, unroll=8)
        for half in range(2):
            got = lax.dot_general(
                ef[first:last, 1024 + half * 128 : 1152 + half * 128], pick[0:span, :], TN, preferred_element_type=F32
            ).astype(BF16)
            for n in range(9):
                for c in range(4):
                    window[((dx + 1) * 9 + n) * 8 + half * 4 + c, 128:160, :] = got[
                        c * 32 : (c + 1) * 32, n * 128 : (n + 1) * 128
                    ]

    source = ec[...].reshape(27 * 16, 1280)
    for c in range(8):
        got = lax.dot_general(
            wcpicks[...], source[:, c * 128 : (c + 1) * 128], NN, preferred_element_type=F32
        ).astype(BF16)
        rest = lax.dot_general(
            wcpicks[...], source[:, 1024 + c * 32 : 1056 + c * 32], NN, preferred_element_type=F32
        )
        rest = jnp.concatenate([rest] * 4, axis=1).astype(BF16)
        group_of_lane = lax.broadcasted_iota(jnp.int32, (16, 128), 1) // 32
        for n in range(27):
            cmain[n * 8 + c] = got[n * 16 : (n + 1) * 16]
            for j in range(4):
                only = (group_of_lane == j).astype(F32).astype(BF16)
                crest[j, n * 8 + c] = rest[n * 16 : (n + 1) * 16] * only

    acc[...] = jnp.zeros_like(acc)
    cacc[...] = jnp.zeros_like(cacc)
    def body(i, tab, octs, slots, n, first_tail, first_slot):
        rests = -(-slots // 4)
        cut = slots // 2 + 1 if slots > 8 else slots
        kept = 16 - cut if slots > 8 else rests
        order = [("head", j) for j in range(cut)] + [("tail", g) for g in range(kept)]
        order += [("head", j) for j in range(cut, slots)] + [("tail", g) for g in range(kept, rests)]
        place = {block: number for number, block in enumerate(order)}
        width = len(order) * 128
        at = [(i * slots + j) * (2 + n) for j in range(slots)]
        km = [tab[a] for a in at]
        kk = [tab[a + 1] for a in at]
        members = [range(4 * g, min(4 * g + 4, slots)) for g in range(rests)]

        def span(kind, number):
            return slice(place[kind, number] * 128, place[kind, number] * 128 + 128)

        for j in range(slots):
            lhs[:, span("head", j)] = heads[km[j], 0:Q, :]
        for g in range(rests):
            lhs[:, span("tail", g)] = tails[first_tail + i * rests + g, 0:Q, :]

        def shown(q, blocks):
            o = octs[i * n + q]
            parts = []
            for kind, number in blocks:
                for j in [number] if kind == "head" else members[number]:
                    w = tab[at[j] + 2 + q]
                    m = jnp.broadcast_to(mask[o, pl.ds(kk[j], 1), :], (16, 128)).astype(BF16)
                    if kind == "head":
                        parts.append(window[w, 0:128, :] * jnp.concatenate([m] * 8, axis=0))
                    else:
                        parts.append(window[w, 128:160, :] * jnp.concatenate([m] * 2, axis=0))
                if kind == "tail" and len(members[number]) < 4:
                    parts.append(jnp.zeros((128 - 32 * len(members[number]), 128), BF16))
            return jnp.concatenate(parts, axis=0)

        for q in range(0, n, PAIR):
            got = None
            for first in range(0, width, DEEP):
                last = min(first + DEEP, width)
                blocks = order[first // 128 : last // 128]
                masked = jnp.concatenate([shown(q + h, blocks) for h in range(PAIR)], axis=1)
                term = lax.dot_general(lhs[:, first:last], masked, NN, preferred_element_type=F32)
                got = term if got is None else got + term
            for h in range(PAIR):
                acc[octs[i * n + q + h]] += got[:, h * 128 : h * 128 + 128]

        total = jnp.zeros((Q, 128), F32)
        for j in range(slots):
            first = (first_slot + i * slots + j) * 8
            ws = [tc[first + q] for q in range(8)]
            seen = jnp.concatenate(
                [
                    jnp.concatenate([cmain[w] for w in ws], axis=0),
                    jnp.concatenate([crest[j % 4, w] for w in ws], axis=0),
                ],
                axis=1,
            )
            both = jnp.concatenate([lhs[:, span("head", j)], lhs[:, span("tail", j // 4)]], axis=1)
            term = lax.dot_general(both, seen, NT, preferred_element_type=F32)
            total += term * cmask[pl.ds(kk[j], 1), :]
        cacc[...] += total

    def eight(i, _):
        for step, planes in enumerate(((1,), (2, 3), (4,), (5, 0, 6))):

            @pl.when(i == step)
            def _(planes=planes):
                for n in planes:
                    loads[n].wait()

        body(i, t8, o8, 25, 8, 0, 0)
        return 0

    load_tails.wait()
    lax.fori_loop(0, 4, eight, 0)

    def four(i, _):
        body(i, t4, o4, 25, 4, 28, 100)
        return 0

    lax.fori_loop(0, 6, four, 0)

    def two(i, _):
        body(i, t2, o2, 8, 2, 70, 250)
        return 0

    lax.fori_loop(0, 12, two, 0, unroll=2)

    local = lax.dot_general(
        (0.5 * cacc[...]).astype(BF16), picks, NN, preferred_element_type=F32
    ).astype(BF16)
    for o in range(8):
        total = acc[o] + lax.dot_general(down[o], local, NN, preferred_element_type=F32)
        density = lax.dot_general(inverse[...], total.astype(BF16), NN, preferred_element_type=F32)
        lhs[:, o * 128 : (o + 1) * 128] = density.astype(BF16)
    out[...] = lax.dot_general(lhs[:, 0:1024], perm[...], NT, preferred_element_type=F32).astype(BF16)


def translate(ef, ec, heads, tails, fine_lists, coarse_lists, down, inverse):
    vmem = pl.BlockSpec(memory_space=pltpu.VMEM)
    smem = pl.BlockSpec(memory_space=pltpu.SMEM)
    tables = [jnp.asarray(part) for members in (EIGHT, FOUR, TWO) for part in table(members)]
    return pl.pallas_call(
        translate_kernel,
        out_shape=jax.ShapeDtypeStruct((Q, 1024), BF16),
        in_specs=[smem] * 7 + [vmem] * 2 + [pl.BlockSpec(memory_space=pl.ANY)] * 2 + [vmem] * 8,
        out_specs=vmem,
        scratch_shapes=[
            pltpu.VMEM((OFFS + 4, 160, 128), BF16),
            pltpu.VMEM((len(TAILS), 160, 128), BF16),
            pltpu.VMEM((448, 1152), BF16),
            pltpu.VMEM((216, 160, 128), BF16),
            pltpu.VMEM((216, 16, 128), BF16),
            pltpu.VMEM((4, 216, 16, 128), BF16),
            pltpu.VMEM((8, OFFS + 4, 128), F32),
            pltpu.VMEM((OFFS + 4, 128), F32),
            pltpu.VMEM((1024, 1024), BF16),
            pltpu.VMEM((Q, 4096), BF16),
            pltpu.VMEM((8, Q, 128), F32),
            pltpu.VMEM((Q, 128), F32),
            pltpu.SemaphoreType.DMA((8,)),
        ],
        compiler_params=pltpu.CompilerParams(vmem_limit_bytes=62 << 20),
        name="translate",
    )(
        *tables, jnp.asarray(coarse_table()), ef, ec, heads, tails, fine_lists, coarse_lists, down, inverse,
        jnp.asarray(window_rows().reshape(1, -1)), jnp.asarray(coarse_window_picks(), BF16),
        jnp.asarray(fine_places()), jnp.asarray(coarse_picks().reshape(8, 16, 128), BF16),
    )


def local(multipole, upward_maps, transfer_maps, downward_maps, check_inverse, fine_lists, coarse_lists):
    ef, ec, heads, tails = exchange(multipole, upward_maps, transfer_maps)
    return translate(ef, ec, heads, tails, fine_lists, coarse_lists, downward_maps, check_inverse)


def solution(mesh):
    placed = (P(None, "curve"), P(), P(), P(), P(), P(None, "curve"), P(None, "curve"))
    return jax.shard_map(local, mesh=mesh, in_specs=placed, out_specs=P(None, "curve"), check_vma=False)
```
